512 devices in a mesh: dp: 16 (over y, x), mp: 32 (over z, core).
Axes of the slice: x: 4, y: 4, z: 16, core: 2. Of those that a mesh axis runs over, the one named last changes fastest.
Arguments:
- temporal: bfloat16 [16384, 4096], P('dp', 'mp'), may hold values from -6 to 6
- code_ids: int32 [16384, 7], P('dp'), may hold values from 0 to 2047
- context_weight: bfloat16 [4096, 1024], P('mp'), may hold values from -0.09375 to 0.09375
- code_tables: bfloat16 [7, 2048, 1024], P(None, None, 'mp'), may hold values from -6 to 6
- gate_proj: bfloat16 [1024, 1536], P(None, 'mp'), may hold values from -0.1875 to 0.1875
- up_proj: bfloat16 [1024, 1536], P(None, 'mp'), may hold values from -0.1875 to 0.1875
- down_proj: bfloat16 [1536, 1024], P('mp'), may hold values from -0.15625 to 0.15625
- out_grad: bfloat16 [16384, 8, 1024], P(('dp', 'mp')), may hold values from -6 to 6
Outputs:
- depth_out: bfloat16 [16384, 8, 1024], P(('dp', 'mp'))
- temporal_grad: bfloat16 [16384, 4096], P('dp', 'mp')
- context_grad: float32 [4096, 1024], P('mp', 'dp')
The draws below stay inside these ranges and needn't reach their ends.
All inputs are finite; a program needn't handle non-finite values.
Results may differ from the reference program's by a relative error of at most 0.025.
Values may be sent and summed in bfloat16 or wider, within the bound.
A program may use at most 64 MiB of HBM per device.

```python
import jax
import jax.numpy as jnp
from jax import lax

DT = 4096
DD = 1024
FF = 1536
VOCAB = 2048
LEVELS = 8
STEP_GRP = 1024
STEPS = 16384
N_DP = 16
N_MP = 32


def set_ends(drawn, rng, smallest, largest):
    longest = drawn.shape.index(max(drawn.shape))
    spots = []
    for shift in (0, 1):
        where = [jax.random.randint(jax.random.fold_in(rng, axis), (), 0, length) for axis, length in enumerate(drawn.shape)]
        where[longest] = (where[longest] + shift) % drawn.shape[longest]
        spots.append(tuple(where))
    return drawn.at[spots[0]].set(smallest).at[spots[1]].set(largest)


def level_of(key, extent, pieces, least, top_value):
    def one(dim, shards_of):
        steps = jax.random.uniform(jax.random.fold_in(jax.random.fold_in(key, 6), dim), (shards_of,), jnp.float32, least / len(pieces), top_value / len(pieces))
        return jnp.repeat(jnp.exp(steps), extent[dim] // shards_of).reshape((-1,) + (1,) * (len(extent) - dim - 1))

    gain = one(*pieces[0])
    for cut in pieces[1:]:
        gain = gain * one(*cut)
    return gain


def bell_draw(stream_key, dims, spread, reach, cuts=(), kind=jnp.bfloat16):
    array = spread * jax.random.normal(stream_key, dims, jnp.float32)
    if cuts:
        array = array * level_of(stream_key, dims, cuts, -0.22, 0.18)
    return jnp.clip(array, -reach, reach).astype(kind)


def setup_inputs(seed: int = 0) -> dict:
    keys = jax.random.split(jax.random.key(seed), 9)
    temporal = bell_draw(keys[0], (STEPS, DT), 1.0, 6.0, ((0, 16), (1, 32)))
    code_ids = set_ends(jax.random.randint(keys[1], (STEPS, LEVELS - 1), 0, VOCAB), jax.random.fold_in(keys[1], 1), 0, VOCAB - 1).astype(jnp.int32)
    context_weight = bell_draw(keys[2], (DT, DD), DT ** -0.5, 0.09375, ((0, 32),))
    code_tables = bell_draw(keys[3], (LEVELS - 1, VOCAB, DD), 1.0, 6.0, ((2, 32),))
    gate_proj = bell_draw(keys[4], (DD, FF), DD ** -0.5, 0.1875, ((1, 32),))
    up_proj = bell_draw(keys[5], (DD, FF), DD ** -0.5, 0.1875, ((1, 32),))
    down_proj = bell_draw(keys[6], (FF, DD), FF ** -0.5, 0.15625, ((0, 32),))
    out_grad = bell_draw(keys[7], (STEPS, LEVELS, DD), 1.0, 6.0, ((0, 512),))
    return dict(temporal=temporal, code_ids=code_ids, context_weight=context_weight, code_tables=code_tables, gate_proj=gate_proj, up_proj=up_proj, down_proj=down_proj, out_grad=out_grad)


def context_sum(temporal, context_weight):
    shard_width = DT // N_MP

    def add_part(total, part_index):
        row_block = lax.dynamic_slice_in_dim(temporal, part_index * shard_width, shard_width, 1)
        weight_block = lax.dynamic_slice_in_dim(context_weight, part_index * shard_width, shard_width, 0)
        part = jnp.dot(row_block, weight_block, preferred_element_type=jnp.float32).astype(jnp.bfloat16)
        part = lax.optimization_barrier(part)
        return (total + part.astype(jnp.float32), None)
    start_total = jnp.zeros((temporal.shape[0], DD), jnp.float32)
    total, unused = lax.scan(add_part, start_total, jnp.arange(N_MP, dtype=jnp.int32))
    return total

def depth_block(inputs, out_grad, gate_proj, up_proj, down_proj):
    meansq = lax.optimization_barrier(jnp.mean(inputs * inputs, axis=-1, keepdims=True))
    inv_rms = lax.rsqrt(meansq + 1e-06)
    normed = inputs * inv_rms
    normed_low = normed.astype(jnp.bfloat16)
    gate_act = jnp.dot(normed_low, gate_proj, preferred_element_type=jnp.float32)
    upper = jnp.dot(normed_low, up_proj, preferred_element_type=jnp.float32)
    sigmoid_gate = jax.nn.sigmoid(gate_act)
    hidden = (gate_act * sigmoid_gate * upper).astype(jnp.bfloat16)
    branch = jnp.dot(hidden, down_proj, preferred_element_type=jnp.float32)
    output = (inputs + branch).astype(jnp.bfloat16)
    hidden_grad = jnp.dot(out_grad, down_proj.T, preferred_element_type=jnp.float32)
    gate_grad = (hidden_grad * upper * sigmoid_gate * (1.0 + gate_act * (1.0 - sigmoid_gate))).astype(jnp.bfloat16)
    up_grad = (hidden_grad * gate_act * sigmoid_gate).astype(jnp.bfloat16)
    normed_grad = jnp.dot(gate_grad, gate_proj.T, preferred_element_type=jnp.float32)
    normed_grad = normed_grad + jnp.dot(up_grad, up_proj.T, preferred_element_type=jnp.float32)
    input_grad = out_grad.astype(jnp.float32) + inv_rms * (normed_grad - normed * lax.optimization_barrier(jnp.mean(normed_grad * normed, axis=-1, keepdims=True)))
    return (output, input_grad)

def reference(temporal, code_ids, context_weight, code_tables, gate_proj, up_proj, down_proj, out_grad):
    context = context_sum(temporal, context_weight)
    flat_tables = code_tables.reshape((LEVELS - 1) * VOCAB, DD)
    offsets = jnp.arange(LEVELS - 1, dtype=jnp.int32) * VOCAB

    def one_group(blocks):
        group_context, group_codes, group_grad = blocks
        embedded = flat_tables[group_codes + offsets[None, :]]
        leading = jnp.zeros((STEP_GRP, 1, DD), jnp.bfloat16)
        inputs = jnp.concatenate([leading, embedded], axis=1).astype(jnp.float32) + group_context[:, None, :]
        output, input_grad = depth_block(inputs.reshape(STEP_GRP * LEVELS, DD), group_grad.reshape(STEP_GRP * LEVELS, DD), gate_proj, up_proj, down_proj)
        context_back = lax.optimization_barrier(jnp.sum(input_grad.reshape(STEP_GRP, LEVELS, DD), axis=1)).astype(jnp.bfloat16)
        return (output.reshape(STEP_GRP, LEVELS, DD), context_back)
    outputs, context_back = lax.map(one_group, (context.reshape(N_DP, STEP_GRP, DD), code_ids.reshape(N_DP, STEP_GRP, LEVELS - 1), out_grad.reshape(N_DP, STEP_GRP, LEVELS, DD)))
    depth_out = outputs.reshape(STEPS, LEVELS, DD)
    context_back = context_back.reshape(STEPS, DD)
    temporal_grad = jnp.dot(context_back, context_weight.T, preferred_element_type=jnp.float32).astype(jnp.bfloat16)
    context_grad = jnp.dot(temporal.T, context_back, preferred_element_type=jnp.float32) / STEP_GRP
    return (depth_out, temporal_grad, context_grad)
```

```python
import functools

import jax
import jax.numpy as jnp
from jax import lax
from jax.experimental import pallas as pl
from jax.experimental.pallas import tpu as pltpu
from jax.sharding import PartitionSpec as P

NX = 4
LANES = 128
BF16 = jnp.bfloat16
F32 = jnp.float32
MESH = pl.DeviceIdType.MESH


def dot_t(left, right):
    return lax.dot_general(left, right, (((1,), (1,)), ((), ())), preferred_element_type=F32)


def dot(left, right):
    return lax.dot_general(left, right, (((1,), (0,)), ((), ())), preferred_element_type=F32)


def copy_to(src, dst, send, recv, device):
    return pltpu.make_async_remote_copy(
        src_ref=src, dst_ref=dst, send_sem=send, recv_sem=recv, device_id=device, device_id_type=MESH
    )


def kernel(
    n_dp, n_mp,
    temporal, codes, ctx_weight, tables, gate_t, up_t, down, out_grad,
    out, temporal_grad, context_grad,
    wall, tx, wx, sums, rs_s, rs_r, xs, yb, rr, ctx, ctx_s, temporal_t,
    inp, nrm, nlow, inv, hid, ngrad, cback, cg_s, cg_r,
    z_s, z_r, x1_s, x1_r, x2_s, x2_r, y_s, y_r, c_s, c_r, rsum_s, rsum_r,
    a2a_s, a2a_r, gz_s, gz_r, gc_s, gc_r, dp_s, dp_r, ex_s, ex_r,
):
    nz = n_mp // 2
    nh = nz // 2
    ny = n_dp // NX
    dp, mp = lax.axis_index("dp"), lax.axis_index("mp")
    x, y = lax.rem(dp, NX), lax.div(dp, NX)
    z, c = lax.div(mp, 2), lax.rem(mp, 2)
    o = 1 - c
    par = lax.rem(y, 2)
    steps = temporal.shape[0]
    sdev = steps // n_mp
    width = ctx_weight.shape[1]
    half = width // 2
    rows = 8 * sdev
    unit = gate_t.shape[0]
    ff = wall.shape[1]

    def wrap(v, n):
        return lax.rem(v + 2 * n, n)

    def at_z(zz, cc):
        return (dp, wrap(zz, nz) * 2 + cc)

    def at_plane(yy, xx):
        return (wrap(yy, ny) * NX + wrap(xx, NX), mp)

    zp, zm = at_z(z + 1, c), at_z(z - 1, c)
    xp, xm = at_plane(y, x + 1), at_plane(y, x - 1)
    yp, ym = at_plane(y + 1, x), at_plane(y - 1, x)
    other = (dp, z * 2 + o)

    barrier = pltpu.get_barrier_semaphore()

    def greet_mp(k, carry):
        pl.semaphore_signal(barrier, inc=1, device_id=(dp, lax.rem(mp + k, n_mp)), device_id_type=MESH)
        return carry

    def greet_dp(k, carry):
        pl.semaphore_signal(barrier, inc=1, device_id=(lax.rem(dp + k, n_dp), mp), device_id_type=MESH)
        return carry

    lax.fori_loop(1, n_mp, greet_mp, 0)
    lax.fori_loop(1, n_dp, greet_dp, 0)

    def w_at(cc, zs, lane, count):
        row = pl.multiple_of((cc * nz + wrap(zs, nz)) * unit, 16)
        return wall.at[:, pl.ds(row, unit), pl.ds(pl.multiple_of(lane, LANES), count)]

    def tile_of(xx):
        return (par * NX + wrap(xx, NX)) * LANES

    mine = tile_of(x)
    row0 = pl.multiple_of((c * nz + z) * unit, 16)
    lane0 = pl.multiple_of(mine, LANES)
    for index, shard in enumerate((gate_t, up_t, down)):
        wall[index, pl.ds(row0, unit), pl.ds(lane0, LANES)] = shard[:, pl.ds(lane0, LANES)]

    pl.semaphore_wait(barrier, n_mp - 1 + n_dp - 1)

    def origin(d, i):
        return z - 1 - i if d == 0 else z + i

    def w_z(d, i, cc):
        zs = origin(d, i)
        return lambda k: copy_to(
            w_at(cc, zs, mine, LANES), w_at(cc, zs, mine, LANES), z_s.at[d * nh + k], z_r.at[d * nh + k],
            zp if d == 0 else zm,
        )

    half_lane = pl.multiple_of(c * half, LANES)
    other_lane = pl.multiple_of(o * half, LANES)
    feat = temporal.shape[1]
    own_feat = pl.multiple_of(c * feat, LANES)
    ex_t = copy_to(temporal, tx.at[:, pl.ds(own_feat, feat)], ex_s.at[0], ex_r.at[0], other)
    ex_w = copy_to(
        ctx_weight.at[:, pl.ds(other_lane, half)], wx.at[pl.ds(own_feat, feat), :], ex_s.at[1], ex_r.at[1], other
    )
    ex_t.start()
    ex_w.start()
    w_z(0, -1, c)(0).start()
    tx[:, pl.ds(own_feat, feat)] = temporal[...]
    wx[pl.ds(own_feat, feat), :] = ctx_weight[:, pl.ds(half_lane, half)]

    groups = n_mp // 4

    def lookup(level, carry):
        code = codes[pl.ds(level, 1), :]
        low = jnp.bitwise_and(code, 255)
        high = lax.shift_right_logical(code, 8)
        table = tables[level]
        parts = table.shape[1] // 256
        stacked = jnp.concatenate([table[:, a * 256 : (a + 1) * 256] for a in range(parts)], axis=0)
        lane = pl.multiple_of(level * LANES, LANES)
        per = min(256, steps)
        for q in range(steps // per):
            piece = slice(q * per, (q + 1) * per)
            hot = (lax.broadcasted_iota(jnp.int32, (256, per), 0) == low[:, piece]).astype(F32).astype(BF16)
            picked = dot(stacked, hot)
            fsize = table.shape[0]
            total = jnp.zeros((fsize, per), F32)
            for a in range(parts):
                total = total + jnp.where(high[:, piece] == a, picked[a * fsize : (a + 1) * fsize, :], 0.0)
            total = total.astype(BF16)
            for e in range(per // LANES):
                g = q * (per // LANES) + e
                xs[g * fsize : (g + 1) * fsize, pl.ds(lane, LANES)] = total[:, e * LANES : (e + 1) * LANES]
        return carry

    levels = codes.shape[0]
    lax.fori_loop(0, levels, lookup, 0)
    for level in range(levels, 8):
        xs[:, level * LANES : (level + 1) * LANES] = jnp.zeros((xs.shape[0], LANES), BF16)
    r_id = lax.broadcasted_iota(jnp.int32, (512, 512), 0)
    c_id = lax.broadcasted_iota(jnp.int32, (512, 512), 1)
    moved = (
        jnp.bitwise_and(lax.shift_right_logical(r_id, 5), 3) * 128
        + lax.shift_right_logical(r_id, 7) * 32
        + jnp.bitwise_and(r_id, 31)
    )
    perm = (moved == c_id).astype(F32).astype(BF16)
    fsize = tables.shape[1]
    for h in range(2):
        spread = dot(xs[:, h * 512 : (h + 1) * 512], perm).astype(BF16)
        for g in range(groups):
            for e in range(4):
                yb[4 * g + e, :, h * LANES : (h + 1) * LANES] = spread[
                    g * fsize : (g + 1) * fsize, e * LANES : (e + 1) * LANES
                ]

    def a2a(target):
        return copy_to(yb.at[target], rr.at[mp], a2a_s.at[target], a2a_r.at[mp], (dp, target))

    a2a(z * 2 + o).start()
    rr[mp] = yb[mp]

    ex_t.wait_recv()
    ex_w.wait_recv()
    chunk = min(256, steps)

    def term(k, carry):
        at = pl.ds(pl.multiple_of(k * chunk, chunk), chunk)
        sums[at, :] = dot(tx[at, :], wx[...])
        return carry

    lax.fori_loop(0, steps // chunk, term, 0)

    chip = 2 * sdev

    def term_of(zd):
        return sums[pl.ds(pl.multiple_of(wrap(zd, nz) * chip, 16), chip), :]

    def ring_sum(d, i):
        k = d * nh + i
        return copy_to(rs_s.at[k], rs_r.at[k], rsum_s.at[k], rsum_r.at[k], zp if d == 0 else zm)

    def dest(d, i):
        return z + (nh - 1) - i if d == 0 else z - nh + i

    for d in (0, 1):
        rs_s[d * nh] = term_of(dest(d, 0)).astype(BF16)
        ring_sum(d, 0).start()

    def w_x1(d, side, i):
        k = (d * 2 + side) * nh + i
        block = w_at(c, origin(d, i), mine, LANES)
        return copy_to(block, block, x1_s.at[k], x1_r.at[k], xp if side == 0 else xm)

    def w_x2(d, i):
        block = w_at(c, origin(d, i), tile_of(x - 1 if d == 0 else x + 1), LANES)
        return copy_to(block, block, x2_s.at[d * nh + i], x2_r.at[d * nh + i], xp if d == 0 else xm)

    def w_y(d, i):
        block = w_at(c, origin(d, i), par * NX * LANES, NX * LANES)
        return copy_to(block, block, y_s.at[d * nh + i], y_r.at[d * nh + i], yp if d == 0 else ym)

    def w_c(d, i, cc):
        block = w_at(cc, origin(d, i), 0, width)
        return copy_to(block, block, c_s.at[d * nh + i], c_r.at[d * nh + i], other)

    def early(i, carry):
        for d in (0, 1):
            last = nh - 2 if d == 0 else nh - 1

            @pl.when(i < last)
            def _():
                ring_sum(d, i).wait_recv()
                rs_s[d * nh + i + 1] = (
                    term_of(dest(d, i + 1)) + rs_r[d * nh + i].astype(F32)
                ).astype(BF16)
                ring_sum(d, i + 1).start()

        @pl.when(i == nh)
        def _():
            ring_sum(0, nh - 2).wait_recv()
            ring_sum(1, nh - 1).wait_recv()
            total = term_of(z) + rs_r[nh - 2].astype(F32) + rs_r[2 * nh - 1].astype(F32)
            first = c == 0
            ctx[:, pl.ds(half_lane, half)] = jnp.where(first, total[:sdev], total[sdev:])
            ctx_s[...] = jnp.where(first, total[sdev:], total[:sdev])
            copy_to(ctx_s, ctx.at[:, pl.ds(half_lane, half)], ex_s.at[2], ex_r.at[2], other).start()

        @pl.when(i < nh)
        def _():
            w_z(0, i, c)(i).wait_recv()

            @pl.when(i > 0)
            def _():
                w_z(1, i, c)(i).wait_recv()

            @pl.when(i < nh - 1)
            def _():
                w_z(0, i, c)(i + 1).start()
                w_z(1, i, c)(i + 1).start()

            for d in (0, 1):
                for side in (0, 1):
                    w_x1(d, side, i).start()

            for cc in (0, 1):
                a2a(wrap(z + nh - i, nz) * 2 + cc).start()

            @pl.when(i > 0)
            def _():
                for cc in (0, 1):
                    a2a(wrap(z - nh + i, nz) * 2 + cc).start()

        @pl.when(jnp.logical_and(i >= 1, i < nh + 1))
        def _():
            for d in (0, 1):
                for side in (0, 1):
                    w_x1(d, side, i - 1).wait_recv()
            for d in (0, 1):
                w_x2(d, i - 1).start()

        @pl.when(jnp.logical_and(i >= 2, i < nh + 2))
        def _():
            for d in (0, 1):
                w_x2(d, i - 2).wait_recv()
                w_y(d, i - 2).start()

        @pl.when(i >= 3)
        def _():
            for d in (0, 1):
                w_y(d, i - 3).wait_recv()
                w_c(d, i - 3, c).start()

        return carry

    lax.fori_loop(0, nh + 3, early, 0)

    temporal_t[...] = temporal[...].astype(F32).T.astype(BF16)

    def await_a2a(k, carry):
        copy_to(yb.at[k], rr.at[k], a2a_s.at[k], a2a_r.at[k], other).wait_recv()
        return carry

    lax.fori_loop(0, mp, await_a2a, 0)
    lax.fori_loop(mp + 1, n_mp, await_a2a, 0)
    copy_to(ctx_s, ctx.at[:, pl.ds(other_lane, half)], ex_s.at[2], ex_r.at[2], other).wait_recv()

    p_row = lax.broadcasted_iota(jnp.int32, (rows, 256), 0)
    p_col = lax.broadcasted_iota(jnp.int32, (rows, 256), 1)
    p_lane = (jnp.bitwise_and(p_row, 7) - 1) * 32 + lax.shift_right_logical(p_row, 3)
    place = (p_lane == p_col).astype(F32).astype(BF16)
    inp[...] = dot_t(place, rr[...].reshape(n_mp * fsize, 256))

    part = 64

    def normalise(k, carry):
        at = pl.ds(pl.multiple_of(k * part, part), part)
        base = ctx[pl.ds(pl.multiple_of(k * (part // 8), 8), part // 8), :]
        value = inp[at, :] + jnp.broadcast_to(base[:, None, :], (part // 8, 8, width)).reshape(part, width)
        scale = lax.rsqrt(jnp.mean(value * value, axis=-1, keepdims=True) + 1e-06)
        normed = value * scale
        inp[at, :] = value
        nrm[at, :] = normed
        nlow[at, :] = normed.astype(BF16)
        inv[at, :] = jnp.broadcast_to(scale, (part, LANES))
        ngrad[at, :] = jnp.zeros((part, width), F32)
        return carry

    lax.fori_loop(0, rows // part, normalise, 0)

    def await_w(k, carry):
        for d in (0, 1):
            w_c(d, k, o).wait_recv()
        return carry

    lax.fori_loop(0, nh, await_w, 0)

    fchunk = 256 if ff % 256 == 0 else 128

    def depth(k, carry):
        at = pl.ds(pl.multiple_of(k * fchunk, fchunk), fchunk)
        gate = dot_t(nlow[...], wall[0, at, :])
        upper = dot_t(nlow[...], wall[1, at, :])
        hgrad = dot_t(out_grad[...], wall[2, at, :])
        sig = jax.nn.sigmoid(gate)
        act = gate * sig
        hid[:, at] = (act * upper).astype(BF16)
        ggrad = (hgrad * upper * sig * (1.0 + gate * (1.0 - sig))).astype(BF16)
        ugrad = (hgrad * act).astype(BF16)
        ngrad[...] += dot(ggrad, wall[0, at, :]) + dot(ugrad, wall[1, at, :])
        return carry

    lax.fori_loop(0, ff // fchunk, depth, 0)

    def back(k, carry):
        at = pl.ds(pl.multiple_of(k * 128, 128), 128)
        grad, normed = ngrad[at, :], nrm[at, :]
        inner = jnp.mean(grad * normed, axis=-1, keepdims=True)
        total = out_grad[at, :].astype(F32) + inv[at, :1] * (grad - normed * inner)
        summed = jnp.sum(total.reshape(16, 8, width), axis=1)
        cback[pl.ds(pl.multiple_of(mp * sdev + k * 16, 16), 16), :] = summed.astype(BF16)
        return carry

    lax.fori_loop(0, rows // 128, back, 0)

    def g_at(zs, cc):
        return cback.at[pl.ds(pl.multiple_of((wrap(zs, nz) * 2 + cc) * sdev, 16), sdev), :]

    def g_z(d, i, k):
        block = g_at(origin(d, i), c)
        return copy_to(block, block, gz_s.at[d * nh + k], gz_r.at[d * nh + k], zp if d == 0 else zm)

    def g_c(d, i, cc):
        block = g_at(origin(d, i), cc)
        return copy_to(block, block, gc_s.at[d * nh + i], gc_r.at[d * nh + i], other)

    g_z(0, -1, 0).start()
    inv_n = 1.0 / steps
    n_chunks = width // 256

    def late(i, carry):
        @pl.when(i > 0)
        def _():
            g_z(0, i - 1, i - 1).wait_recv()

            @pl.when(i < nh)
            def _():
                g_z(0, i - 1, i).start()

            g_c(0, i - 1, c).start()

        @pl.when(i < nh)
        def _():
            @pl.when(i > 0)
            def _():
                g_z(1, i, i).wait_recv()

            @pl.when(i < nh - 1)
            def _():
                g_z(1, i, i + 1).start()

            g_c(1, i, c).start()

        @pl.when(i < n_chunks)
        def _():
            at = pl.ds(pl.multiple_of(i * 256, 256), 256)
            out[:, at] = (inp[:, at] + dot(hid[...], wall[2, :, at])).astype(BF16)

        return carry

    lax.fori_loop(0, nh + 1, late, 0)

    def await_g(k, carry):
        for d in (0, 1):
            g_c(d, k, o).wait_recv()
        return carry

    lax.fori_loop(0, nh, await_g, 0)

    cols = width // n_dp
    cg_s[...] = (dot(temporal_t[...], cback[...]) * inv_n).T.astype(BF16)

    def cg(target):
        block = cg_s.at[pl.ds(pl.multiple_of(target * cols, 16), cols), :]
        return copy_to(block, cg_r.at[dp], dp_s.at[target], dp_r.at[dp], (target, mp))

    def send_cg(k, carry):
        cg(lax.rem(dp + k, n_dp)).start()
        return carry

    lax.fori_loop(1, n_dp, send_cg, 0)
    cg_r[dp] = cg_s[pl.ds(pl.multiple_of(dp * cols, 16), cols), :]

    def tgrad(k, carry):
        at = pl.ds(pl.multiple_of(k * chunk, chunk), chunk)
        temporal_grad[at, :] = dot_t(cback[at, :], ctx_weight[...]).astype(BF16)
        return carry

    lax.fori_loop(0, steps // chunk, tgrad, 0)

    ex_t.wait_send()
    ex_w.wait_send()
    copy_to(ctx_s, ctx.at[:, pl.ds(half_lane, half)], ex_s.at[2], ex_r.at[2], other).wait_send()

    def sent(i, carry):
        w_z(0, i, c)(i).wait_send()
        g_z(0, i, i).wait_send()
        ring_sum(1, i).wait_send()

        @pl.when(i > 0)
        def _():
            w_z(1, i, c)(i).wait_send()
            g_z(1, i, i).wait_send()

        @pl.when(i < nh - 1)
        def _():
            ring_sum(0, i).wait_send()

        for d in (0, 1):
            for side in (0, 1):
                w_x1(d, side, i).wait_send()
            w_x2(d, i).wait_send()
            w_y(d, i).wait_send()
            w_c(d, i, c).wait_send()
            g_c(d, i, c).wait_send()
        return carry

    lax.fori_loop(0, nh, sent, 0)

    def sent_a2a(k, carry):
        a2a(lax.rem(mp + k, n_mp)).wait_send()
        return carry

    lax.fori_loop(1, n_mp, sent_a2a, 0)

    def await_cg(k, carry):
        source = lax.rem(dp + k, n_dp)
        copy_to(cg_r.at[source], cg_r.at[source], dp_s.at[source], dp_r.at[source], other).wait_recv()
        cg(source).wait_send()
        return carry

    lax.fori_loop(1, n_dp, await_cg, 0)
    total = cg_r[0].astype(F32)
    for k in range(1, n_dp):
        total = total + cg_r[k].astype(F32)
    context_grad[...] = total


def per_device(
    n_dp, n_mp, temporal, code_ids, context_weight, code_tables, gate_proj, up_proj, down_proj, out_grad
):
    steps, feat = temporal.shape
    sdev, levels, width = out_grad.shape
    rows = sdev * levels
    unit = down_proj.shape[0]
    ff = unit * n_mp
    nh = n_mp // 4
    cols = width // n_dp
    half = width // 2
    fsize = code_tables.shape[2]
    vmem = pl.BlockSpec(memory_space=pltpu.VMEM)
    dma = lambda n: pltpu.SemaphoreType.DMA((n,))
    scratch = [
        pltpu.VMEM((3, ff, width), BF16),
        pltpu.VMEM((steps, 2 * feat), BF16),
        pltpu.VMEM((2 * feat, half), BF16),
        pltpu.VMEM((steps, half), F32),
        pltpu.VMEM((2 * nh, 2 * sdev, half), BF16),
        pltpu.VMEM((2 * nh, 2 * sdev, half), BF16),
        pltpu.VMEM((fsize * n_mp // 4, 8 * LANES), BF16),
        pltpu.VMEM((n_mp, fsize, 256), BF16),
        pltpu.VMEM((n_mp, fsize, 256), BF16),
        pltpu.VMEM((sdev, width), F32),
        pltpu.VMEM((sdev, half), F32),
        pltpu.VMEM((feat, steps), BF16),
        pltpu.VMEM((rows, width), F32),
        pltpu.VMEM((rows, width), F32),
        pltpu.VMEM((rows, width), BF16),
        pltpu.VMEM((rows, LANES), F32),
        pltpu.VMEM((rows, ff), BF16),
        pltpu.VMEM((rows, width), F32),
        pltpu.VMEM((steps, width), BF16),
        pltpu.VMEM((width, feat), BF16),
        pltpu.VMEM((n_dp, cols, feat), BF16),
    ]
    sems = [2 * nh, 4 * nh, 2 * nh, 2 * nh, 2 * nh, 2 * nh, n_mp, 2 * nh, 2 * nh, n_dp, 3]
    for n in sems:
        scratch += [dma(n), dma(n)]
    out, tgrad, cgrad = pl.pallas_call(
        functools.partial(kernel, n_dp, n_mp),
        out_shape=(
            jax.ShapeDtypeStruct((rows, width), BF16),
            jax.ShapeDtypeStruct((steps, feat), BF16),
            jax.ShapeDtypeStruct((cols, feat), F32),
        ),
        in_specs=[vmem] * 8,
        out_specs=(vmem, vmem, vmem),
        scratch_shapes=scratch,
        compiler_params=pltpu.CompilerParams(
            collective_id=0, has_side_effects=True, vmem_limit_bytes=58 * 1024 * 1024
        ),
        cost_estimate=pl.CostEstimate(
            flops=2 * rows * width * ff * 6 + 6 * steps * feat * width, bytes_accessed=4 * 2**20, transcendentals=0
        ),
        name="depth_block",
    )(
        temporal,
        code_ids.T,
        context_weight,
        code_tables.transpose(0, 2, 1),
        gate_proj.T,
        up_proj.T,
        down_proj,
        out_grad.reshape(rows, width),
    )
    return out.reshape(sdev, levels, width), tgrad, cgrad.T


def solution(mesh):
    in_specs = (
        P("dp", "mp"),
        P("dp", None),
        P("mp", None),
        P(None, None, "mp"),
        P(None, "mp"),
        P(None, "mp"),
        P("mp", None),
        P(("dp", "mp"), None, None),
    )
    out_specs = (P(("dp", "mp"), None, None), P("dp", "mp"), P("mp", "dp"))
    return jax.shard_map(
        functools.partial(per_device, mesh.shape["dp"], mesh.shape["mp"]),
        mesh=mesh,
        in_specs=in_specs,
        out_specs=out_specs,
        check_vma=False,
    )
```

```python
import functools

import jax
import jax.numpy as jnp
from jax import lax
from jax.experimental import pallas as pl
from jax.experimental.pallas import tpu as pltpu
from jax.sharding import PartitionSpec as P

NX = 4
LANES = 128
BF16 = jnp.bfloat16
F32 = jnp.float32
MESH = pl.DeviceIdType.MESH


def dot_t(left, right):
    return lax.dot_general(left, right, (((1,), (1,)), ((), ())), preferred_element_type=F32)


def dot(left, right):
    return lax.dot_general(left, right, (((1,), (0,)), ((), ())), preferred_element_type=F32)


def copy_to(src, dst, send, recv, device):
    return pltpu.make_async_remote_copy(
        src_ref=src, dst_ref=dst, send_sem=send, recv_sem=recv, device_id=device, device_id_type=MESH
    )


def kernel(
    n_dp, n_mp,
    temporal, codes, ctx_weight, tables, gate_t, up_t, down, out_grad,
    out, temporal_grad, context_grad,
    wall, tx, wx, sums, rs_s, rs_r, xs, yb, rr, ctx, ctx_s, temporal_t,
    inp, nrm, nlow, inv, hid, hback, ngrad, cback, cg_s, cg_r,
    z_s, z_r, x1_s, x1_r, x2_s, x2_r, y_s, y_r, c_s, c_r, rsum_s, rsum_r,
    a2a_s, a2a_r, gz_s, gz_r, gc_s, gc_r, dp_s, dp_r, ex_s, ex_r,
):
    nz = n_mp // 2
    nh = nz // 2
    ny = n_dp // NX
    dp, mp = lax.axis_index("dp"), lax.axis_index("mp")
    x, y = lax.rem(dp, NX), lax.div(dp, NX)
    z, c = lax.div(mp, 2), lax.rem(mp, 2)
    o = 1 - c
    par = lax.rem(y, 2)
    steps = temporal.shape[0]
    sdev = steps // n_mp
    width = ctx_weight.shape[1]
    half = width // 2
    rows = 8 * sdev
    unit = gate_t.shape[0]
    ff = wall.shape[1]

    def wrap(v, n):
        return lax.rem(v + 2 * n, n)

    def at_z(zz, cc):
        return (dp, wrap(zz, nz) * 2 + cc)

    def at_plane(yy, xx):
        return (wrap(yy, ny) * NX + wrap(xx, NX), mp)

    zp, zm = at_z(z + 1, c), at_z(z - 1, c)
    xp, xm = at_plane(y, x + 1), at_plane(y, x - 1)
    yp, ym = at_plane(y + 1, x), at_plane(y - 1, x)
    other = (dp, z * 2 + o)

    barrier = pltpu.get_barrier_semaphore()

    def greet_mp(k, carry):
        pl.semaphore_signal(barrier, inc=1, device_id=(dp, lax.rem(mp + k, n_mp)), device_id_type=MESH)
        return carry

    def greet_dp(k, carry):
        pl.semaphore_signal(barrier, inc=1, device_id=(lax.rem(dp + k, n_dp), mp), device_id_type=MESH)
        return carry

    lax.fori_loop(1, n_mp, greet_mp, 0)
    lax.fori_loop(1, n_dp, greet_dp, 0)

    def w_at(cc, zs, lane, count):
        row = pl.multiple_of((cc * nz + wrap(zs, nz)) * unit, 16)
        return wall.at[:, pl.ds(row, unit), pl.ds(pl.multiple_of(lane, LANES), count)]

    def tile_of(xx):
        return (par * NX + wrap(xx, NX)) * LANES

    mine = tile_of(x)
    row0 = pl.multiple_of((c * nz + z) * unit, 16)
    lane0 = pl.multiple_of(mine, LANES)
    for index, shard in enumerate((gate_t, up_t, down)):
        wall[index, pl.ds(row0, unit), pl.ds(lane0, LANES)] = shard[:, pl.ds(lane0, LANES)]

    pl.semaphore_wait(barrier, n_mp - 1 + n_dp - 1)

    def origin(d, i):
        return z - 1 - i if d == 0 else z + i

    def w_z(d, i, cc):
        zs = origin(d, i)
        return lambda k: copy_to(
            w_at(cc, zs, mine, LANES), w_at(cc, zs, mine, LANES), z_s.at[d * nh + k], z_r.at[d * nh + k],
            zp if d == 0 else zm,
        )

    half_lane = pl.multiple_of(c * half, LANES)
    other_lane = pl.multiple_of(o * half, LANES)
    feat = temporal.shape[1]
    own_feat = pl.multiple_of(c * feat, LANES)
    ex_t = copy_to(temporal, tx.at[:, pl.ds(own_feat, feat)], ex_s.at[0], ex_r.at[0], other)
    ex_w = copy_to(
        ctx_weight.at[:, pl.ds(other_lane, half)], wx.at[pl.ds(own_feat, feat), :], ex_s.at[1], ex_r.at[1], other
    )
    ex_t.start()
    ex_w.start()
    w_z(0, -1, c)(0).start()
    tx[:, pl.ds(own_feat, feat)] = temporal[...]
    wx[pl.ds(own_feat, feat), :] = ctx_weight[:, pl.ds(half_lane, half)]

    groups = n_mp // 4

    def lookup(level, carry):
        code = codes[pl.ds(level, 1), :]
        low = jnp.bitwise_and(code, 255)
        high = lax.shift_right_logical(code, 8)
        table = tables[level]
        parts = table.shape[1] // 256
        stacked = jnp.concatenate([table[:, a * 256 : (a + 1) * 256] for a in range(parts)], axis=0)
        lane = pl.multiple_of(level * LANES, LANES)
        per = min(256, steps)
        for q in range(steps // per):
            piece = slice(q * per, (q + 1) * per)
            hot = (lax.broadcasted_iota(jnp.int32, (256, per), 0) == low[:, piece]).astype(F32).astype(BF16)
            picked = dot(stacked, hot)
            total = jnp.zeros((fsize, per), F32)
            for a in range(parts):
                total = total + jnp.where(high[:, piece] == a, picked[a * fsize : (a + 1) * fsize, :], 0.0)
            total = total.astype(BF16)
            for e in range(per // LANES):
                g = q * (per // LANES) + e
                xs[g * fsize : (g + 1) * fsize, pl.ds(lane, LANES)] = total[:, e * LANES : (e + 1) * LANES]
        return carry

    levels = codes.shape[0]
    fsize = tables.shape[1]

    def arrange():
        for level in range(levels, 8):
            xs[:, level * LANES : (level + 1) * LANES] = jnp.zeros((xs.shape[0], LANES), BF16)
        r_id = lax.broadcasted_iota(jnp.int32, (512, 512), 0)
        c_id = lax.broadcasted_iota(jnp.int32, (512, 512), 1)
        moved = (
            jnp.bitwise_and(lax.shift_right_logical(r_id, 5), 3) * 128
            + lax.shift_right_logical(r_id, 7) * 32
            + jnp.bitwise_and(r_id, 31)
        )
        perm = (moved == c_id).astype(F32).astype(BF16)
        for h in range(2):
            spread = dot(xs[:, h * 512 : (h + 1) * 512], perm).astype(BF16)
            for g in range(groups):
                for e in range(4):
                    yb[4 * g + e, :, h * LANES : (h + 1) * LANES] = spread[
                        g * fsize : (g + 1) * fsize, e * LANES : (e + 1) * LANES
                    ]
        rr[mp] = yb[mp]

    def a2a(target):
        return copy_to(yb.at[target], rr.at[mp], a2a_s.at[target], a2a_r.at[mp], (dp, target))

    temporal_t[...] = temporal[...].astype(F32).T.astype(BF16)
    ex_t.wait_recv()
    ex_w.wait_recv()
    chunk = min(256, steps)

    def term(k, carry):
        at = pl.ds(pl.multiple_of(k * chunk, chunk), chunk)
        sums[at, :] = dot(tx[at, :], wx[...])
        return carry

    lax.fori_loop(0, steps // chunk, term, 0)

    chip = 2 * sdev

    def term_of(zd):
        return sums[pl.ds(pl.multiple_of(wrap(zd, nz) * chip, 16), chip), :]

    def ring_sum(d, i):
        k = d * nh + i
        return copy_to(rs_s.at[k], rs_r.at[k], rsum_s.at[k], rsum_r.at[k], zp if d == 0 else zm)

    def dest(d, i):
        return z + (nh - 1) - i if d == 0 else z - nh + i

    for d in (0, 1):
        rs_s[d * nh] = term_of(dest(d, 0)).astype(BF16)
        ring_sum(d, 0).start()

    def w_x1(d, side, i):
        k = (d * 2 + side) * nh + i
        block = w_at(c, origin(d, i), mine, LANES)
        return copy_to(block, block, x1_s.at[k], x1_r.at[k], xp if side == 0 else xm)

    def w_x2(d, i):
        block = w_at(c, origin(d, i), tile_of(x - 1 if d == 0 else x + 1), LANES)
        return copy_to(block, block, x2_s.at[d * nh + i], x2_r.at[d * nh + i], xp if d == 0 else xm)

    def w_y(d, i):
        block = w_at(c, origin(d, i), par * NX * LANES, NX * LANES)
        return copy_to(block, block, y_s.at[d * nh + i], y_r.at[d * nh + i], yp if d == 0 else ym)

    def w_c(d, i, cc):
        block = w_at(cc, origin(d, i), 0, width)
        return copy_to(block, block, c_s.at[d * nh + i], c_r.at[d * nh + i], other)

    first_send = nh // 2

    def early(i, carry):
        for d in (0, 1):
            last = nh - 2 if d == 0 else nh - 1

            @pl.when(i < last)
            def _():
                ring_sum(d, i).wait_recv()
                rs_s[d * nh + i + 1] = (
                    term_of(dest(d, i + 1)) + rs_r[d * nh + i].astype(F32)
                ).astype(BF16)
                ring_sum(d, i + 1).start()

        @pl.when(i == nh)
        def _():
            ring_sum(0, nh - 2).wait_recv()
            ring_sum(1, nh - 1).wait_recv()
            total = term_of(z) + rs_r[nh - 2].astype(F32) + rs_r[2 * nh - 1].astype(F32)
            first = c == 0
            ctx[:, pl.ds(half_lane, half)] = jnp.where(first, total[:sdev], total[sdev:])
            ctx_s[...] = jnp.where(first, total[sdev:], total[:sdev])
            copy_to(ctx_s, ctx.at[:, pl.ds(half_lane, half)], ex_s.at[2], ex_r.at[2], other).start()

        @pl.when(i < nh)
        def _():
            w_z(0, i, c)(i).wait_recv()

            @pl.when(i > 0)
            def _():
                w_z(1, i, c)(i).wait_recv()

            @pl.when(i < nh - 1)
            def _():
                w_z(0, i, c)(i + 1).start()
                w_z(1, i, c)(i + 1).start()

            for d in (0, 1):
                for side in (0, 1):
                    w_x1(d, side, i).start()

        @pl.when(jnp.logical_and(i >= 1, i < nh + 1))
        def _():
            for d in (0, 1):
                for side in (0, 1):
                    w_x1(d, side, i - 1).wait_recv()
            for d in (0, 1):
                w_x2(d, i - 1).start()

        @pl.when(jnp.logical_and(i >= 2, i < nh + 2))
        def _():
            for d in (0, 1):
                w_x2(d, i - 2).wait_recv()
                w_y(d, i - 2).start()

        @pl.when(i >= 3)
        def _():
            for d in (0, 1):
                w_y(d, i - 3).wait_recv()
                w_c(d, i - 3, c).start()

        @pl.when(i < first_send)
        def _():
            lax.fori_loop(2 * i, jnp.minimum(2 * i + 2, levels), lookup, 0)

        @pl.when(i == first_send - 1)
        def _():
            arrange()

        @pl.when(i == first_send)
        def _():
            a2a(z * 2 + o).start()

        @pl.when(jnp.logical_and(i >= first_send, i < nh))
        def _():
            for e in (0, 1):
                apart = nh - 2 * (i - first_send) - e
                for cc in (0, 1):
                    a2a(wrap(z + apart, nz) * 2 + cc).start()

                @pl.when(apart < nh)
                def _():
                    for cc in (0, 1):
                        a2a(wrap(z - apart, nz) * 2 + cc).start()

        return carry

    lax.fori_loop(0, nh + 3, early, 0)

    def await_w(k, carry):
        for d in (0, 1):
            w_c(d, k, o).wait_recv()
        return carry

    lax.fori_loop(0, nh, await_w, 0)

    fchunk = 256 if ff % 256 == 0 else 128

    def hidden_back(k, carry):
        at = pl.ds(pl.multiple_of(k * fchunk, fchunk), fchunk)
        hback[:, at] = dot_t(out_grad[...], wall[2, at, :])
        return carry

    lax.fori_loop(0, ff // fchunk, hidden_back, 0)

    def await_a2a(k, carry):
        copy_to(yb.at[k], rr.at[k], a2a_s.at[k], a2a_r.at[k], other).wait_recv()
        return carry

    lax.fori_loop(0, mp, await_a2a, 0)
    lax.fori_loop(mp + 1, n_mp, await_a2a, 0)
    copy_to(ctx_s, ctx.at[:, pl.ds(other_lane, half)], ex_s.at[2], ex_r.at[2], other).wait_recv()

    p_row = lax.broadcasted_iota(jnp.int32, (rows, 256), 0)
    p_col = lax.broadcasted_iota(jnp.int32, (rows, 256), 1)
    p_lane = (jnp.bitwise_and(p_row, 7) - 1) * 32 + lax.shift_right_logical(p_row, 3)
    place = (p_lane == p_col).astype(F32).astype(BF16)
    inp[...] = dot_t(place, rr[...].reshape(n_mp * fsize, 256))

    part = 64

    def normalise(k, carry):
        at = pl.ds(pl.multiple_of(k * part, part), part)
        base = ctx[pl.ds(pl.multiple_of(k * (part // 8), 8), part // 8), :]
        value = inp[at, :] + jnp.broadcast_to(base[:, None, :], (part // 8, 8, width)).reshape(part, width)
        scale = lax.rsqrt(jnp.mean(value * value, axis=-1, keepdims=True) + 1e-06)
        normed = value * scale
        inp[at, :] = value
        nrm[at, :] = normed
        nlow[at, :] = normed.astype(BF16)
        inv[at, :] = jnp.broadcast_to(scale, (part, LANES))
        ngrad[at, :] = jnp.zeros((part, width), F32)
        return carry

    lax.fori_loop(0, rows // part, normalise, 0)

    def depth(k, carry):
        at = pl.ds(pl.multiple_of(k * fchunk, fchunk), fchunk)
        gate = dot_t(nlow[...], wall[0, at, :])
        upper = dot_t(nlow[...], wall[1, at, :])
        hgrad = hback[:, at]
        sig = jax.nn.sigmoid(gate)
        act = gate * sig
        hid[:, at] = (act * upper).astype(BF16)
        ggrad = (hgrad * upper * sig * (1.0 + gate * (1.0 - sig))).astype(BF16)
        ugrad = (hgrad * act).astype(BF16)
        ngrad[...] += dot(ggrad, wall[0, at, :]) + dot(ugrad, wall[1, at, :])
        return carry

    lax.fori_loop(0, ff // fchunk, depth, 0)

    part_g = sdev // 2

    def g_rows(zs, cc, first, count):
        return cback.at[pl.ds(pl.multiple_of((wrap(zs, nz) * 2 + cc) * sdev + first, 16), count), :]

    def g_z(d, i, k, h):
        block = g_rows(origin(d, i), c, h * part_g, part_g)
        at = (d * nh + k) * 2 + h
        return copy_to(block, block, gz_s.at[at], gz_r.at[at], zp if d == 0 else zm)

    def g_c(d, i, cc):
        block = g_rows(origin(d, i), cc, 0, sdev)
        return copy_to(block, block, gc_s.at[d * nh + i], gc_r.at[d * nh + i], other)

    def back(k, carry):
        at = pl.ds(pl.multiple_of(k * (rows // 2), rows // 2), rows // 2)
        grad, normed = ngrad[at, :], nrm[at, :]
        inner = jnp.mean(grad * normed, axis=-1, keepdims=True)
        total = out_grad[at, :].astype(F32) + inv[at, :1] * (grad - normed * inner)
        summed = jnp.sum(total.reshape(part_g, 8, width), axis=1)
        cback[pl.ds(pl.multiple_of(mp * sdev + k * part_g, 16), part_g), :] = summed.astype(BF16)
        g_z(0, -1, 0, k).start()
        g_z(1, 0, 1, k).start()
        return carry

    lax.fori_loop(0, 2, back, 0)

    inv_n = 1.0 / steps
    n_chunks = width // 256

    def late(i, carry):
        for h in (0, 1):

            @pl.when(i > 0)
            def _():
                g_z(0, i - 1, i - 1, h).wait_recv()

                @pl.when(i < nh)
                def _():
                    g_z(0, i - 1, i, h).start()

            @pl.when(jnp.logical_and(i > 0, i < nh))
            def _():
                g_z(1, i, i, h).wait_recv()

                @pl.when(i < nh - 1)
                def _():
                    g_z(1, i, i + 1, h).start()

        @pl.when(i > 0)
        def _():
            g_c(0, i - 1, c).start()

        @pl.when(i < nh)
        def _():
            g_c(1, i, c).start()

        @pl.when(i < n_chunks)
        def _():
            at = pl.ds(pl.multiple_of(i * 256, 256), 256)
            out[:, at] = (inp[:, at] + dot(hid[...], wall[2, :, at])).astype(BF16)

        return carry

    lax.fori_loop(0, nh + 1, late, 0)

    def await_g(k, carry):
        for d in (0, 1):
            g_c(d, k, o).wait_recv()
        return carry

    lax.fori_loop(0, nh, await_g, 0)

    cols = width // n_dp
    cg_s[...] = (dot(temporal_t[...], cback[...]) * inv_n).T.astype(BF16)

    def cg(target):
        block = cg_s.at[pl.ds(pl.multiple_of(target * cols, 16), cols), :]
        return copy_to(block, cg_r.at[dp], dp_s.at[target], dp_r.at[dp], (target, mp))

    def send_cg(k, carry):
        cg(lax.rem(dp + k, n_dp)).start()
        return carry

    lax.fori_loop(1, n_dp, send_cg, 0)
    cg_r[dp] = cg_s[pl.ds(pl.multiple_of(dp * cols, 16), cols), :]

    def tgrad(k, carry):
        at = pl.ds(pl.multiple_of(k * chunk, chunk), chunk)
        temporal_grad[at, :] = dot_t(cback[at, :], ctx_weight[...]).astype(BF16)
        return carry

    lax.fori_loop(0, steps // chunk, tgrad, 0)

    ex_t.wait_send()
    ex_w.wait_send()
    copy_to(ctx_s, ctx.at[:, pl.ds(half_lane, half)], ex_s.at[2], ex_r.at[2], other).wait_send()

    def sent(i, carry):
        w_z(0, i, c)(i).wait_send()
        for h in (0, 1):
            g_z(0, i, i, h).wait_send()
        ring_sum(1, i).wait_send()

        @pl.when(i > 0)
        def _():
            w_z(1, i, c)(i).wait_send()
            for h in (0, 1):
                g_z(1, i, i, h).wait_send()

        @pl.when(i < nh - 1)
        def _():
            ring_sum(0, i).wait_send()

        for d in (0, 1):
            for side in (0, 1):
                w_x1(d, side, i).wait_send()
            w_x2(d, i).wait_send()
            w_y(d, i).wait_send()
            w_c(d, i, c).wait_send()
            g_c(d, i, c).wait_send()
        return carry

    lax.fori_loop(0, nh, sent, 0)

    def sent_a2a(k, carry):
        a2a(lax.rem(mp + k, n_mp)).wait_send()
        return carry

    lax.fori_loop(1, n_mp, sent_a2a, 0)

    def await_cg(k, carry):
        source = lax.rem(dp + k, n_dp)
        copy_to(cg_r.at[source], cg_r.at[source], dp_s.at[source], dp_r.at[source], other).wait_recv()
        cg(source).wait_send()
        return carry

    lax.fori_loop(1, n_dp, await_cg, 0)
    total = cg_r[0].astype(F32)
    for k in range(1, n_dp):
        total = total + cg_r[k].astype(F32)
    context_grad[...] = total


def hand_over(a, b, d, a_out, b_out, d_out, sems):
    copies = [
        pltpu.make_async_copy(src, dst, sems.at[k])
        for k, (src, dst) in enumerate(((a, a_out), (b, b_out), (d, d_out)))
    ]
    for copy in copies:
        copy.start()
    for copy in copies:
        copy.wait()


def per_device(
    n_dp, n_mp, temporal, code_ids, context_weight, code_tables, gate_proj, up_proj, down_proj, out_grad
):
    steps, feat = temporal.shape
    sdev, levels, width = out_grad.shape
    rows = sdev * levels
    unit = down_proj.shape[0]
    ff = unit * n_mp
    nh = n_mp // 4
    cols = width // n_dp
    half = width // 2
    fsize = code_tables.shape[2]
    vmem = pl.BlockSpec(memory_space=pltpu.VMEM)
    dma = lambda n: pltpu.SemaphoreType.DMA((n,))
    scratch = [
        pltpu.VMEM((3, ff, width), BF16),
        pltpu.VMEM((steps, 2 * feat), BF16),
        pltpu.VMEM((2 * feat, half), BF16),
        pltpu.VMEM((steps, half), F32),
        pltpu.VMEM((2 * nh, 2 * sdev, half), BF16),
        pltpu.VMEM((2 * nh, 2 * sdev, half), BF16),
        pltpu.VMEM((fsize * n_mp // 4, 8 * LANES), BF16),
        pltpu.VMEM((n_mp, fsize, 256), BF16),
        pltpu.VMEM((n_mp, fsize, 256), BF16),
        pltpu.VMEM((sdev, width), F32),
        pltpu.VMEM((sdev, half), F32),
        pltpu.VMEM((feat, steps), BF16),
        pltpu.VMEM((rows, width), F32),
        pltpu.VMEM((rows, width), F32),
        pltpu.VMEM((rows, width), BF16),
        pltpu.VMEM((rows, LANES), F32),
        pltpu.VMEM((rows, ff), BF16),
        pltpu.VMEM((rows, ff), F32),
        pltpu.VMEM((rows, width), F32),
        pltpu.VMEM((steps, width), BF16),
        pltpu.VMEM((width, feat), BF16),
        pltpu.VMEM((n_dp, cols, feat), BF16),
    ]
    sems = [2 * nh, 4 * nh, 2 * nh, 2 * nh, 2 * nh, 2 * nh, n_mp, 4 * nh, 2 * nh, n_dp, 3]
    for n in sems:
        scratch += [dma(n), dma(n)]
    out, tgrad, cgrad = pl.pallas_call(
        functools.partial(kernel, n_dp, n_mp),
        out_shape=(
            jax.ShapeDtypeStruct((rows, width), BF16),
            jax.ShapeDtypeStruct((steps, feat), BF16),
            jax.ShapeDtypeStruct((cols, feat), F32),
        ),
        in_specs=[vmem] * 8,
        out_specs=(vmem, vmem, vmem),
        scratch_shapes=scratch,
        compiler_params=pltpu.CompilerParams(
            collective_id=0, has_side_effects=True, vmem_limit_bytes=58 * 1024 * 1024
        ),
        cost_estimate=pl.CostEstimate(
            flops=2 * rows * width * ff * 6 + 6 * steps * feat * width, bytes_accessed=4 * 2**20, transcendentals=0
        ),
        name="depth_block",
    )(
        temporal,
        code_ids.T,
        context_weight,
        code_tables.transpose(0, 2, 1),
        gate_proj.T,
        up_proj.T,
        down_proj,
        out_grad.reshape(rows, width),
    )
    anywhere = pl.BlockSpec(memory_space=pl.ANY)
    out, tgrad, cgrad = pl.pallas_call(
        hand_over,
        out_shape=tuple(jax.ShapeDtypeStruct(v.shape, v.dtype) for v in (out, tgrad, cgrad)),
        in_specs=[anywhere] * 3,
        out_specs=(anywhere,) * 3,
        scratch_shapes=[dma(3)],
        name="hand_over",
    )(out, tgrad, cgrad)
    return out.reshape(sdev, levels, width), tgrad, cgrad.T


def solution(mesh):
    in_specs = (
        P("dp", "mp"),
        P("dp", None),
        P("mp", None),
        P(None, None, "mp"),
        P(None, "mp"),
        P(None, "mp"),
        P("mp", None),
        P(("dp", "mp"), None, None),
    )
    out_specs = (P(("dp", "mp"), None, None), P("dp", "mp"), P("mp", "dp"))
    return jax.shard_map(
        functools.partial(per_device, mesh.shape["dp"], mesh.shape["mp"]),
        mesh=mesh,
        in_specs=in_specs,
        out_specs=out_specs,
        check_vma=False,
    )
```

```python
import functools

import jax
import jax.numpy as jnp
from jax import lax
from jax.experimental import pallas as pl
from jax.experimental.pallas import tpu as pltpu
from jax.sharding import PartitionSpec as P

NX = 4
LANES = 128
BF16 = jnp.bfloat16
F32 = jnp.float32
MESH = pl.DeviceIdType.MESH


def dot_t(left, right):
    return lax.dot_general(left, right, (((1,), (1,)), ((), ())), preferred_element_type=F32)


def dot(left, right):
    return lax.dot_general(left, right, (((1,), (0,)), ((), ())), preferred_element_type=F32)


def copy_to(src, dst, send, recv, device):
    return pltpu.make_async_remote_copy(
        src_ref=src, dst_ref=dst, send_sem=send, recv_sem=recv, device_id=device, device_id_type=MESH
    )


def swap_blocks(v):
    lane = lax.broadcasted_iota(jnp.int32, v[0].shape, 1)
    low = lane < 64
    even = jnp.bitwise_and(lane, 32) == 0
    w = [None] * 4
    for a in (0, 1):
        w[a] = jnp.where(low, v[a], pltpu.roll(v[a + 2], 64, 1))
        w[a + 2] = jnp.where(low, pltpu.roll(v[a], 64, 1), v[a + 2])
    out = [None] * 4
    for a in (0, 2):
        out[a] = jnp.where(even, w[a], pltpu.roll(w[a + 1], 32, 1))
        out[a + 1] = jnp.where(even, pltpu.roll(w[a], 96, 1), w[a + 1])
    return out


def kernel(
    n_dp, n_mp,
    temporal, codes, ctx_weight, tables, gate_t, up_t, down, out_grad,
    out, temporal_grad, context_grad,
    wall, tx, wx, sums, rs_s, rs_r, yb, rr, relay, ctx, ctx_s, temporal_t,
    inp, nrm, nlow, inv, hid, hback, ngrad, cback, cg_s, cg_r,
    z_s, z_r, x1_s, x1_r, x2_s, x2_r, y_s, y_r, c_s, c_r, rsum_s, rsum_r,
    a2a_s, a2a_r, gz_s, gz_r, gc_s, gc_r, dp_s, dp_r, ex_s, ex_r, rl_s, rl_r,
):
    nz = n_mp // 2
    nh = nz // 2
    ny = n_dp // NX
    dp, mp = lax.axis_index("dp"), lax.axis_index("mp")
    x, y = lax.rem(dp, NX), lax.div(dp, NX)
    z, c = lax.div(mp, 2), lax.rem(mp, 2)
    o = 1 - c
    par = lax.rem(y, 2)
    steps = temporal.shape[0]
    sdev = steps // n_mp
    width = ctx_weight.shape[1]
    half = width // 2
    rows = 8 * sdev
    unit = gate_t.shape[0]
    ff = wall.shape[1]

    def wrap(v, n):
        return lax.rem(v + 2 * n, n)

    def at_z(zz, cc):
        return (dp, wrap(zz, nz) * 2 + cc)

    def at_plane(yy, xx):
        return (wrap(yy, ny) * NX + wrap(xx, NX), mp)

    zp, zm = at_z(z + 1, c), at_z(z - 1, c)
    xp, xm = at_plane(y, x + 1), at_plane(y, x - 1)
    yp, ym = at_plane(y + 1, x), at_plane(y - 1, x)
    other = (dp, z * 2 + o)

    barrier = pltpu.get_barrier_semaphore()

    def greet_mp(k, carry):
        pl.semaphore_signal(barrier, inc=1, device_id=(dp, lax.rem(mp + k, n_mp)), device_id_type=MESH)
        return carry

    def greet_dp(k, carry):
        pl.semaphore_signal(barrier, inc=1, device_id=(lax.rem(dp + k, n_dp), mp), device_id_type=MESH)
        return carry

    lax.fori_loop(1, n_mp, greet_mp, 0)
    lax.fori_loop(1, n_dp, greet_dp, 0)

    def w_at(cc, zs, lane, count):
        row = pl.multiple_of((cc * nz + wrap(zs, nz)) * unit, 16)
        return wall.at[:, pl.ds(row, unit), pl.ds(pl.multiple_of(lane, LANES), count)]

    def tile_of(xx):
        return (par * NX + wrap(xx, NX)) * LANES

    mine = tile_of(x)
    row0 = pl.multiple_of((c * nz + z) * unit, 16)
    lane0 = pl.multiple_of(mine, LANES)
    for index, shard in enumerate((gate_t, up_t, down)):
        wall[index, pl.ds(row0, unit), pl.ds(lane0, LANES)] = shard[:, pl.ds(lane0, LANES)]

    pl.semaphore_wait(barrier, n_mp - 1 + n_dp - 1)

    def origin(d, i):
        return z - 1 - i if d == 0 else z + i

    def w_z(d, i, cc):
        zs = origin(d, i)
        return lambda k: copy_to(
            w_at(cc, zs, mine, LANES), w_at(cc, zs, mine, LANES), z_s.at[d * nh + k], z_r.at[d * nh + k],
            zp if d == 0 else zm,
        )

    half_lane = pl.multiple_of(c * half, LANES)
    other_lane = pl.multiple_of(o * half, LANES)
    feat = temporal.shape[1]
    own_feat = pl.multiple_of(c * feat, LANES)
    ex_t = copy_to(temporal, tx.at[:, pl.ds(own_feat, feat)], ex_s.at[0], ex_r.at[0], other)
    ex_w = copy_to(
        ctx_weight.at[:, pl.ds(other_lane, half)], wx.at[pl.ds(own_feat, feat), :], ex_s.at[1], ex_r.at[1], other
    )
    ex_t.start()
    ex_w.start()
    w_z(0, -1, c)(0).start()
    tx[:, pl.ds(own_feat, feat)] = temporal[...]
    wx[pl.ds(own_feat, feat), :] = ctx_weight[:, pl.ds(half_lane, half)]


    def lookup(level, carry):
        code = codes[pl.ds(level, 1), :]
        low = jnp.bitwise_and(code, 255)
        high = lax.shift_right_logical(code, 8)
        table = tables[level]
        parts = table.shape[1] // 256
        stacked = jnp.concatenate([table[:, a * 256 : (a + 1) * 256] for a in range(parts)], axis=0)
        per = min(256, steps)
        for q in range(steps // per):
            piece = slice(q * per, (q + 1) * per)
            hot = (lax.broadcasted_iota(jnp.int32, (256, per), 0) == low[:, piece]).astype(F32).astype(BF16)
            picked = dot(stacked, hot)
            total = jnp.zeros((fsize, per), F32)
            for a in range(parts):
                total = total + jnp.where(high[:, piece] == a, picked[a * fsize : (a + 1) * fsize, :], 0.0)
            for e in range(per // LANES):
                g = q * (per // LANES) + e
                block = total[:, e * LANES : (e + 1) * LANES]
                tiles = swap_blocks([block[8 * a : 8 * a + 8] for a in range(4)])
                for a in range(4):
                    yb[4 * g + a, level] = tiles[a].astype(BF16)
        return carry

    levels = codes.shape[0]
    fsize = tables.shape[1]

    def a2a(target):
        return copy_to(yb.at[target], rr.at[mp], a2a_s.at[target], a2a_r.at[mp], (dp, target))

    quarter = nh // 2

    def leg_one(cc):
        target = wrap(z + nh, nz) * 2 + cc
        over = z + quarter if cc == 0 else z - quarter
        return copy_to(yb.at[target], relay.at[cc], a2a_s.at[target], rl_r.at[cc], at_z(over, c))

    def leg_two(cc):
        source, over = (z - quarter, z + quarter) if cc == 0 else (z + quarter, z - quarter)
        origin_mp = wrap(source, nz) * 2 + c
        return copy_to(relay.at[cc], rr.at[origin_mp], rl_s.at[cc], a2a_r.at[origin_mp], at_z(over, cc))

    def await_leg(cc):
        copy_to(relay.at[cc], relay.at[cc], rl_s.at[cc], rl_r.at[cc], other).wait_recv()

    temporal_t[...] = temporal[...].astype(F32).T.astype(BF16)
    ex_t.wait_recv()
    ex_w.wait_recv()
    chunk = min(256, steps)

    def term(k, carry):
        at = pl.ds(pl.multiple_of(k * chunk, chunk), chunk)
        sums[at, :] = dot(tx[at, :], wx[...])
        return carry

    lax.fori_loop(0, steps // chunk, term, 0)

    chip = 2 * sdev

    def term_of(zd):
        return sums[pl.ds(pl.multiple_of(wrap(zd, nz) * chip, 16), chip), :]

    def ring_sum(d, i):
        k = d * nh + i
        return copy_to(rs_s.at[k], rs_r.at[k], rsum_s.at[k], rsum_r.at[k], zp if d == 0 else zm)

    def dest(d, i):
        return z + (nh - 1) - i if d == 0 else z - nh + i

    for d in (0, 1):
        rs_s[d * nh] = term_of(dest(d, 0)).astype(BF16)
        ring_sum(d, 0).start()

    def w_x1(d, side, i):
        k = (d * 2 + side) * nh + i
        block = w_at(c, origin(d, i), mine, LANES)
        return copy_to(block, block, x1_s.at[k], x1_r.at[k], xp if side == 0 else xm)

    def w_x2(d, i):
        block = w_at(c, origin(d, i), tile_of(x - 1 if d == 0 else x + 1), LANES)
        return copy_to(block, block, x2_s.at[d * nh + i], x2_r.at[d * nh + i], xp if d == 0 else xm)

    def w_y(d, i):
        block = w_at(c, origin(d, i), par * NX * LANES, NX * LANES)
        return copy_to(block, block, y_s.at[d * nh + i], y_r.at[d * nh + i], yp if d == 0 else ym)

    def w_c(d, i, cc):
        block = w_at(cc, origin(d, i), 0, width)
        return copy_to(block, block, c_s.at[d * nh + i], c_r.at[d * nh + i], other)

    first_send = nh // 2

    def early(i, carry):
        for d in (0, 1):
            last = nh - 2 if d == 0 else nh - 1

            @pl.when(i < last)
            def _():
                ring_sum(d, i).wait_recv()
                rs_s[d * nh + i + 1] = (
                    term_of(dest(d, i + 1)) + rs_r[d * nh + i].astype(F32)
                ).astype(BF16)
                ring_sum(d, i + 1).start()

        @pl.when(i == nh)
        def _():
            ring_sum(0, nh - 2).wait_recv()
            ring_sum(1, nh - 1).wait_recv()
            total = term_of(z) + rs_r[nh - 2].astype(F32) + rs_r[2 * nh - 1].astype(F32)
            first = c == 0
            ctx[:, pl.ds(half_lane, half)] = jnp.where(first, total[:sdev], total[sdev:])
            ctx_s[...] = jnp.where(first, total[sdev:], total[:sdev])
            copy_to(ctx_s, ctx.at[:, pl.ds(half_lane, half)], ex_s.at[2], ex_r.at[2], other).start()

        @pl.when(i < nh)
        def _():
            w_z(0, i, c)(i).wait_recv()

            @pl.when(i > 0)
            def _():
                w_z(1, i, c)(i).wait_recv()

            @pl.when(i < nh - 1)
            def _():
                w_z(0, i, c)(i + 1).start()
                w_z(1, i, c)(i + 1).start()

            for d in (0, 1):
                for side in (0, 1):
                    w_x1(d, side, i).start()

        @pl.when(jnp.logical_and(i >= 1, i < nh + 1))
        def _():
            for d in (0, 1):
                for side in (0, 1):
                    w_x1(d, side, i - 1).wait_recv()
            for d in (0, 1):
                w_x2(d, i - 1).start()

        @pl.when(jnp.logical_and(i >= 2, i < nh + 2))
        def _():
            for d in (0, 1):
                w_x2(d, i - 2).wait_recv()
                w_y(d, i - 2).start()

        @pl.when(i >= 3)
        def _():
            for d in (0, 1):
                w_y(d, i - 3).wait_recv()
                w_c(d, i - 3, c).start()

        @pl.when(i < first_send)
        def _():
            lax.fori_loop(2 * i, jnp.minimum(2 * i + 2, levels), lookup, 0)

        @pl.when(i == first_send - 1)
        def _():
            rr[mp] = yb[mp]

        @pl.when(i == first_send)
        def _():
            a2a(z * 2 + o).start()
            for cc in (0, 1):
                leg_one(cc).start()

        @pl.when(i == nh - 1)
        def _():
            for cc in (0, 1):
                await_leg(cc)
                leg_two(cc).start()

        @pl.when(jnp.logical_and(i >= first_send, i < nh))
        def _():
            for e in (0, 1):
                apart = nh - 2 * (i - first_send) - e

                @pl.when(apart < nh)
                def _():
                    for cc in (0, 1):
                        a2a(wrap(z + apart, nz) * 2 + cc).start()
                        a2a(wrap(z - apart, nz) * 2 + cc).start()

        return carry

    lax.fori_loop(0, nh + 3, early, 0)

    def await_w(k, carry):
        for d in (0, 1):
            w_c(d, k, o).wait_recv()
        return carry

    lax.fori_loop(0, nh, await_w, 0)

    fchunk = 256 if ff % 256 == 0 else 128

    def hidden_back(k, carry):
        at = pl.ds(pl.multiple_of(k * fchunk, fchunk), fchunk)
        hback[:, at] = dot_t(out_grad[...], wall[2, at, :])
        return carry

    lax.fori_loop(0, ff // fchunk, hidden_back, 0)

    def await_a2a(k, carry):
        copy_to(yb.at[k], rr.at[k], a2a_s.at[k], a2a_r.at[k], other).wait_recv()
        return carry

    lax.fori_loop(0, mp, await_a2a, 0)
    lax.fori_loop(mp + 1, n_mp, await_a2a, 0)
    copy_to(ctx_s, ctx.at[:, pl.ds(other_lane, half)], ex_s.at[2], ex_r.at[2], other).wait_recv()

    p_row = lax.broadcasted_iota(jnp.int32, (rows, 256), 0)
    p_col = lax.broadcasted_iota(jnp.int32, (rows, 256), 1)
    p_lane = (jnp.bitwise_and(p_row, 7) - 1) * 32 + lax.shift_right_logical(p_row, 3)
    place = (p_lane == p_col).astype(F32).astype(BF16)

    def place_rows(k, carry):
        at = pl.ds(pl.multiple_of(k * 8, 8), 8)
        sides = []
        for h in range(2):
            tiles = [
                rr[at, l].astype(F32).reshape(64, LANES) if l < levels else jnp.zeros((64, LANES), F32)
                for l in range(4 * h, 4 * h + 4)
            ]
            tiles = [t.reshape(8, 1, 8, LANES) for t in swap_blocks(tiles)]
            sides.append(jnp.concatenate(tiles, axis=1).reshape(256, LANES))
        block = jnp.concatenate(sides, axis=1).astype(BF16)
        inp[:, pl.ds(pl.multiple_of(k * 256, 256), 256)] = dot_t(place, block)
        return carry

    lax.fori_loop(0, n_mp // 8, place_rows, 0)

    part = 64

    def normalise(k, carry):
        at = pl.ds(pl.multiple_of(k * part, part), part)
        base = ctx[pl.ds(pl.multiple_of(k * (part // 8), 8), part // 8), :]
        value = inp[at, :] + jnp.broadcast_to(base[:, None, :], (part // 8, 8, width)).reshape(part, width)
        scale = lax.rsqrt(jnp.mean(value * value, axis=-1, keepdims=True) + 1e-06)
        normed = value * scale
        inp[at, :] = value
        nrm[at, :] = normed
        nlow[at, :] = normed.astype(BF16)
        inv[at, :] = jnp.broadcast_to(scale, (part, LANES))
        ngrad[at, :] = jnp.zeros((part, width), F32)
        return carry

    lax.fori_loop(0, rows // part, normalise, 0)

    def depth(k, carry):
        at = pl.ds(pl.multiple_of(k * fchunk, fchunk), fchunk)
        gate = dot_t(nlow[...], wall[0, at, :])
        upper = dot_t(nlow[...], wall[1, at, :])
        hgrad = hback[:, at]
        sig = jax.nn.sigmoid(gate)
        act = gate * sig
        hid[:, at] = (act * upper).astype(BF16)
        ggrad = (hgrad * upper * sig * (1.0 + gate * (1.0 - sig))).astype(BF16)
        ugrad = (hgrad * act).astype(BF16)
        ngrad[...] += dot(ggrad, wall[0, at, :]) + dot(ugrad, wall[1, at, :])
        return carry

    lax.fori_loop(0, ff // fchunk, depth, 0)

    part_g = sdev // 2

    def g_rows(zs, cc, first, count):
        return cback.at[pl.ds(pl.multiple_of((wrap(zs, nz) * 2 + cc) * sdev + first, 16), count), :]

    def g_z(d, i, k, h):
        block = g_rows(origin(d, i), c, h * part_g, part_g)
        at = (d * nh + k) * 2 + h
        return copy_to(block, block, gz_s.at[at], gz_r.at[at], zp if d == 0 else zm)

    def g_c(d, i, cc):
        block = g_rows(origin(d, i), cc, 0, sdev)
        return copy_to(block, block, gc_s.at[d * nh + i], gc_r.at[d * nh + i], other)

    def back(k, carry):
        at = pl.ds(pl.multiple_of(k * (rows // 2), rows // 2), rows // 2)
        grad, normed = ngrad[at, :], nrm[at, :]
        inner = jnp.mean(grad * normed, axis=-1, keepdims=True)
        total = out_grad[at, :].astype(F32) + inv[at, :1] * (grad - normed * inner)
        summed = jnp.sum(total.reshape(part_g, 8, width), axis=1)
        cback[pl.ds(pl.multiple_of(mp * sdev + k * part_g, 16), part_g), :] = summed.astype(BF16)
        g_z(0, -1, 0, k).start()
        g_z(1, 0, 1, k).start()
        return carry

    lax.fori_loop(0, 2, back, 0)

    inv_n = 1.0 / steps

    def sent_early(i):
        w_z(0, i, c)(i).wait_send()
        ring_sum(1, i).wait_send()

        @pl.when(i > 0)
        def _():
            w_z(1, i, c)(i).wait_send()

        @pl.when(i < nh - 1)
        def _():
            ring_sum(0, i).wait_send()

        for d in (0, 1):
            for side in (0, 1):
                w_x1(d, side, i).wait_send()
            w_x2(d, i).wait_send()
            w_y(d, i).wait_send()
            w_c(d, i, c).wait_send()

        def sent_a2a(k, carry):
            a2a(lax.rem(mp + k, n_mp)).wait_send()
            return carry

        lax.fori_loop(1 + 4 * i, jnp.minimum(5 + 4 * i, n_mp), sent_a2a, 0)

    ex_t.wait_send()
    ex_w.wait_send()
    copy_to(ctx_s, ctx.at[:, pl.ds(half_lane, half)], ex_s.at[2], ex_r.at[2], other).wait_send()
    for cc in (0, 1):
        leg_two(cc).wait_send()
    n_chunks = width // 256

    def late(i, carry):
        for h in (0, 1):

            @pl.when(i > 0)
            def _():
                g_z(0, i - 1, i - 1, h).wait_recv()

                @pl.when(i < nh)
                def _():
                    g_z(0, i - 1, i, h).start()

            @pl.when(jnp.logical_and(i > 0, i < nh))
            def _():
                g_z(1, i, i, h).wait_recv()

                @pl.when(i < nh - 1)
                def _():
                    g_z(1, i, i + 1, h).start()

        @pl.when(i > 0)
        def _():
            g_c(0, i - 1, c).start()

        @pl.when(i < nh)
        def _():
            g_c(1, i, c).start()

        @pl.when(i < n_chunks)
        def _():
            at = pl.ds(pl.multiple_of(i * 256, 256), 256)
            out[:, at] = (inp[:, at] + dot(hid[...], wall[2, :, at])).astype(BF16)

        @pl.when(i < nh)
        def _():
            sent_early(i)

        return carry

    lax.fori_loop(0, nh + 1, late, 0)

    def await_g(k, carry):
        for d in (0, 1):
            g_c(d, k, o).wait_recv()
        return carry

    lax.fori_loop(0, nh, await_g, 0)

    cols = width // n_dp
    cg_s[...] = (dot(temporal_t[...], cback[...]) * inv_n).T.astype(BF16)

    def cg(target):
        block = cg_s.at[pl.ds(pl.multiple_of(target * cols, 16), cols), :]
        return copy_to(block, cg_r.at[dp], dp_s.at[target], dp_r.at[dp], (target, mp))

    def send_cg(k, carry):
        cg(lax.rem(dp + k, n_dp)).start()
        return carry

    lax.fori_loop(1, n_dp, send_cg, 0)
    cg_r[dp] = cg_s[pl.ds(pl.multiple_of(dp * cols, 16), cols), :]

    def tgrad(k, carry):
        at = pl.ds(pl.multiple_of(k * chunk, chunk), chunk)
        temporal_grad[at, :] = dot_t(cback[at, :], ctx_weight[...]).astype(BF16)
        return carry

    lax.fori_loop(0, steps // chunk, tgrad, 0)

    def sent(i, carry):
        for h in (0, 1):
            g_z(0, i, i, h).wait_send()

        @pl.when(i > 0)
        def _():
            for h in (0, 1):
                g_z(1, i, i, h).wait_send()

        for d in (0, 1):
            g_c(d, i, c).wait_send()
        return carry

    lax.fori_loop(0, nh, sent, 0)

    def await_cg(k, carry):
        source = lax.rem(dp + k, n_dp)
        copy_to(cg_r.at[source], cg_r.at[source], dp_s.at[source], dp_r.at[source], other).wait_recv()
        cg(source).wait_send()
        return carry

    lax.fori_loop(1, n_dp, await_cg, 0)
    total = cg_r[0].astype(F32)
    for k in range(1, n_dp):
        total = total + cg_r[k].astype(F32)
    context_grad[...] = total


def hand_over(a, b, d, a_out, b_out, d_out):
    a_out[...] = a[...]
    b_out[...] = b[...]
    d_out[...] = d[...]


def per_device(
    n_dp, n_mp, temporal, code_ids, context_weight, code_tables, gate_proj, up_proj, down_proj, out_grad
):
    steps, feat = temporal.shape
    sdev, levels, width = out_grad.shape
    rows = sdev * levels
    unit = down_proj.shape[0]
    ff = unit * n_mp
    nh = n_mp // 4
    cols = width // n_dp
    half = width // 2
    inputs_levels = code_tables.shape[0]
    vmem = pl.BlockSpec(memory_space=pltpu.VMEM)
    dma = lambda n: pltpu.SemaphoreType.DMA((n,))
    scratch = [
        pltpu.VMEM((3, ff, width), BF16),
        pltpu.VMEM((steps, 2 * feat), BF16),
        pltpu.VMEM((2 * feat, half), BF16),
        pltpu.VMEM((steps, half), F32),
        pltpu.VMEM((2 * nh, 2 * sdev, half), BF16),
        pltpu.VMEM((2 * nh, 2 * sdev, half), BF16),
        pltpu.VMEM((n_mp, inputs_levels, 8, LANES), BF16),
        pltpu.VMEM((n_mp, inputs_levels, 8, LANES), BF16),
        pltpu.VMEM((2, inputs_levels, 8, LANES), BF16),
        pltpu.VMEM((sdev, width), F32),
        pltpu.VMEM((sdev, half), F32),
        pltpu.VMEM((feat, steps), BF16),
        pltpu.VMEM((rows, width), F32),
        pltpu.VMEM((rows, width), F32),
        pltpu.VMEM((rows, width), BF16),
        pltpu.VMEM((rows, LANES), F32),
        pltpu.VMEM((rows, ff), BF16),
        pltpu.VMEM((rows, ff), F32),
        pltpu.VMEM((rows, width), F32),
        pltpu.VMEM((steps, width), BF16),
        pltpu.VMEM((width, feat), BF16),
        pltpu.VMEM((n_dp, cols, feat), BF16),
    ]
    sems = [2 * nh, 4 * nh, 2 * nh, 2 * nh, 2 * nh, 2 * nh, n_mp, 4 * nh, 2 * nh, n_dp, 3, 2]
    for n in sems:
        scratch += [dma(n), dma(n)]
    out, tgrad, cgrad = pl.pallas_call(
        functools.partial(kernel, n_dp, n_mp),
        out_shape=(
            jax.ShapeDtypeStruct((rows, width), BF16),
            jax.ShapeDtypeStruct((steps, feat), BF16),
            jax.ShapeDtypeStruct((cols, feat), F32),
        ),
        in_specs=[vmem] * 8,
        out_specs=(vmem, vmem, vmem),
        scratch_shapes=scratch,
        compiler_params=pltpu.CompilerParams(
            collective_id=0, has_side_effects=True, vmem_limit_bytes=58 * 1024 * 1024
        ),
        cost_estimate=pl.CostEstimate(
            flops=2 * rows * width * ff * 6 + 6 * steps * feat * width, bytes_accessed=4 * 2**20, transcendentals=0
        ),
        name="depth_block",
    )(
        temporal,
        code_ids.T,
        context_weight,
        code_tables.transpose(0, 2, 1),
        gate_proj.T,
        up_proj.T,
        down_proj,
        out_grad.reshape(rows, width),
    )
    out, tgrad, cgrad = pl.pallas_call(
        hand_over,
        out_shape=tuple(jax.ShapeDtypeStruct(v.shape, v.dtype) for v in (out, tgrad, cgrad)),
        in_specs=[vmem] * 3,
        out_specs=(vmem,) * 3,
        name="hand_over",
    )(out, tgrad, cgrad)
    return out.reshape(sdev, levels, width), tgrad, cgrad.T


def solution(mesh):
    in_specs = (
        P("dp", "mp"),
        P("dp", None),
        P("mp", None),
        P(None, None, "mp"),
        P(None, "mp"),
        P(None, "mp"),
        P("mp", None),
        P(("dp", "mp"), None, None),
    )
    out_specs = (P(("dp", "mp"), None, None), P("dp", "mp"), P("mp", "dp"))
    return jax.shard_map(
        functools.partial(per_device, mesh.shape["dp"], mesh.shape["mp"]),
        mesh=mesh,
        in_specs=in_specs,
        out_specs=out_specs,
        check_vma=False,
    )
```

```python
import functools

import jax
import jax.numpy as jnp
from jax import lax
from jax.experimental import pallas as pl
from jax.experimental.pallas import tpu as pltpu
from jax.sharding import PartitionSpec as P

NX = 4
LANES = 128
BF16 = jnp.bfloat16
F32 = jnp.float32
MESH = pl.DeviceIdType.MESH


def dot_t(left, right):
    return lax.dot_general(left, right, (((1,), (1,)), ((), ())), preferred_element_type=F32)


def dot(left, right):
    return lax.dot_general(left, right, (((1,), (0,)), ((), ())), preferred_element_type=F32)


def copy_to(src, dst, send, recv, device):
    return pltpu.make_async_remote_copy(
        src_ref=src, dst_ref=dst, send_sem=send, recv_sem=recv, device_id=device, device_id_type=MESH
    )


def swap_blocks(v):
    lane = lax.broadcasted_iota(jnp.int32, v[0].shape, 1)
    low = lane < 64
    even = jnp.bitwise_and(lane, 32) == 0
    w = [None] * 4
    for a in (0, 1):
        w[a] = jnp.where(low, v[a], pltpu.roll(v[a + 2], 64, 1))
        w[a + 2] = jnp.where(low, pltpu.roll(v[a], 64, 1), v[a + 2])
    out = [None] * 4
    for a in (0, 2):
        out[a] = jnp.where(even, w[a], pltpu.roll(w[a + 1], 32, 1))
        out[a + 1] = jnp.where(even, pltpu.roll(w[a], 96, 1), w[a + 1])
    return out


def kernel(
    n_dp, n_mp,
    temporal, codes, ctx_weight, tables, gate_t, up_t, down, out_grad,
    out, temporal_grad, context_grad,
    wall, tx, wx, sums, rs_s, rs_r, yb, rr, relay, ctx, ctx_s, temporal_t,
    inp, nrm, nlow, inv, hid, hback, ngrad, cback, cg_s, cg_r,
    z_s, z_r, x1_s, x1_r, x2_s, x2_r, y_s, y_r, c_s, c_r, rsum_s, rsum_r,
    a2a_s, a2a_r, gz_s, gz_r, gc_s, gc_r, dp_s, dp_r, ex_s, ex_r, rl_s, rl_r,
):
    nz = n_mp // 2
    nh = nz // 2
    ny = n_dp // NX
    dp, mp = lax.axis_index("dp"), lax.axis_index("mp")
    x, y = lax.rem(dp, NX), lax.div(dp, NX)
    z, c = lax.div(mp, 2), lax.rem(mp, 2)
    o = 1 - c
    par = lax.rem(y, 2)
    steps = temporal.shape[0]
    sdev = steps // n_mp
    width = ctx_weight.shape[1]
    half = width // 2
    rows = 8 * sdev
    unit = gate_t.shape[0]
    ff = wall.shape[1]

    def wrap(v, n):
        return lax.rem(v + 2 * n, n)

    def at_z(zz, cc):
        return (dp, wrap(zz, nz) * 2 + cc)

    def at_plane(yy, xx):
        return (wrap(yy, ny) * NX + wrap(xx, NX), mp)

    zp, zm = at_z(z + 1, c), at_z(z - 1, c)
    xp, xm = at_plane(y, x + 1), at_plane(y, x - 1)
    yp, ym = at_plane(y + 1, x), at_plane(y - 1, x)
    other = (dp, z * 2 + o)

    barrier = pltpu.get_barrier_semaphore()

    def greet_mp(k, carry):
        pl.semaphore_signal(barrier, inc=1, device_id=(dp, lax.rem(mp + k, n_mp)), device_id_type=MESH)
        return carry

    def greet_dp(k, carry):
        pl.semaphore_signal(barrier, inc=1, device_id=(lax.rem(dp + k, n_dp), mp), device_id_type=MESH)
        return carry

    lax.fori_loop(1, n_mp, greet_mp, 0)
    lax.fori_loop(1, n_dp, greet_dp, 0)

    def w_at(cc, zs, lane, count):
        row = pl.multiple_of((cc * nz + wrap(zs, nz)) * unit, 16)
        return wall.at[:, pl.ds(row, unit), pl.ds(pl.multiple_of(lane, LANES), count)]

    def tile_of(xx):
        return (par * NX + wrap(xx, NX)) * LANES

    mine = tile_of(x)
    row0 = pl.multiple_of((c * nz + z) * unit, 16)
    lane0 = pl.multiple_of(mine, LANES)
    for index, shard in enumerate((gate_t, up_t, down)):
        wall[index, pl.ds(row0, unit), pl.ds(lane0, LANES)] = shard[:, pl.ds(lane0, LANES)]

    pl.semaphore_wait(barrier, n_mp - 1 + n_dp - 1)

    def origin(d, i):
        return z - 1 - i if d == 0 else z + i

    def w_z(d, i, cc):
        zs = origin(d, i)
        return lambda k: copy_to(
            w_at(cc, zs, mine, LANES), w_at(cc, zs, mine, LANES), z_s.at[d * nh + k], z_r.at[d * nh + k],
            zp if d == 0 else zm,
        )

    half_lane = pl.multiple_of(c * half, LANES)
    other_lane = pl.multiple_of(o * half, LANES)
    feat = temporal.shape[1]
    own_feat = pl.multiple_of(c * feat, LANES)
    ex_t = copy_to(temporal, tx.at[:, pl.ds(own_feat, feat)], ex_s.at[0], ex_r.at[0], other)
    ex_w = copy_to(
        ctx_weight.at[:, pl.ds(other_lane, half)], wx.at[pl.ds(own_feat, feat), :], ex_s.at[1], ex_r.at[1], other
    )
    ex_t.start()
    ex_w.start()
    w_z(0, -1, c)(0).start()
    tx[:, pl.ds(own_feat, feat)] = temporal[...]
    wx[pl.ds(own_feat, feat), :] = ctx_weight[:, pl.ds(half_lane, half)]


    def lookup(level, carry):
        code = codes[pl.ds(level, 1), :]
        low = jnp.bitwise_and(code, 255)
        high = lax.shift_right_logical(code, 8)
        table = tables[level]
        parts = table.shape[1] // 256
        stacked = jnp.concatenate([table[:, a * 256 : (a + 1) * 256] for a in range(parts)], axis=0)
        per = min(256, steps)
        for q in range(steps // per):
            piece = slice(q * per, (q + 1) * per)
            hot = (lax.broadcasted_iota(jnp.int32, (256, per), 0) == low[:, piece]).astype(F32).astype(BF16)
            picked = dot(stacked, hot)
            total = jnp.zeros((fsize, per), F32)
            for a in range(parts):
                total = total + jnp.where(high[:, piece] == a, picked[a * fsize : (a + 1) * fsize, :], 0.0)
            for e in range(per // LANES):
                g = q * (per // LANES) + e
                block = total[:, e * LANES : (e + 1) * LANES]
                tiles = swap_blocks([block[8 * a : 8 * a + 8] for a in range(4)])
                for a in range(4):
                    yb[4 * g + a, level] = tiles[a].astype(BF16)
        return carry

    levels = codes.shape[0]
    fsize = tables.shape[1]

    def a2a(target):
        return copy_to(yb.at[target], rr.at[mp], a2a_s.at[target], a2a_r.at[mp], (dp, target))

    quarter = nh // 2

    def leg_one(cc):
        target = wrap(z + nh, nz) * 2 + cc
        over = z + quarter if cc == 0 else z - quarter
        return copy_to(yb.at[target], relay.at[cc], a2a_s.at[target], rl_r.at[cc], at_z(over, c))

    def leg_two(cc):
        source, over = (z - quarter, z + quarter) if cc == 0 else (z + quarter, z - quarter)
        origin_mp = wrap(source, nz) * 2 + c
        return copy_to(relay.at[cc], rr.at[origin_mp], rl_s.at[cc], a2a_r.at[origin_mp], at_z(over, cc))

    def await_leg(cc):
        copy_to(relay.at[cc], relay.at[cc], rl_s.at[cc], rl_r.at[cc], other).wait_recv()

    ex_t.wait_recv()
    ex_w.wait_recv()
    chunk = min(256, steps)

    def term(k, carry):
        at = pl.ds(pl.multiple_of(k * chunk, chunk), chunk)
        sums[at, :] = dot(tx[at, :], wx[...])
        return carry

    lax.fori_loop(0, steps // chunk, term, 0)

    chip = 2 * sdev

    def term_of(zd):
        return sums[pl.ds(pl.multiple_of(wrap(zd, nz) * chip, 16), chip), :]

    def ring_sum(d, i):
        k = d * nh + i
        return copy_to(rs_s.at[k], rs_r.at[k], rsum_s.at[k], rsum_r.at[k], zp if d == 0 else zm)

    def dest(d, i):
        return z + (nh - 1) - i if d == 0 else z - nh + i

    for d in (0, 1):
        rs_s[d * nh] = term_of(dest(d, 0)).astype(BF16)
        ring_sum(d, 0).start()

    def w_x1(d, side, i):
        k = (d * 2 + side) * nh + i
        block = w_at(c, origin(d, i), mine, LANES)
        return copy_to(block, block, x1_s.at[k], x1_r.at[k], xp if side == 0 else xm)

    def w_x2(d, i):
        block = w_at(c, origin(d, i), tile_of(x - 1 if d == 0 else x + 1), LANES)
        return copy_to(block, block, x2_s.at[d * nh + i], x2_r.at[d * nh + i], xp if d == 0 else xm)

    def w_y(d, i):
        block = w_at(c, origin(d, i), par * NX * LANES, NX * LANES)
        return copy_to(block, block, y_s.at[d * nh + i], y_r.at[d * nh + i], yp if d == 0 else ym)

    def w_c(d, i, cc):
        block = w_at(cc, origin(d, i), 0, width)
        return copy_to(block, block, c_s.at[d * nh + i], c_r.at[d * nh + i], other)

    first_send = nh // 2
    lag = 2

    def early(i, carry):
        for d in (0, 1):
            last = nh - 2 if d == 0 else nh - 1

            @pl.when(i < last)
            def _():
                ring_sum(d, i).wait_recv()
                rs_s[d * nh + i + 1] = (
                    term_of(dest(d, i + 1)) + rs_r[d * nh + i].astype(F32)
                ).astype(BF16)
                ring_sum(d, i + 1).start()

        @pl.when(i == nh)
        def _():
            ring_sum(0, nh - 2).wait_recv()
            ring_sum(1, nh - 1).wait_recv()
            total = term_of(z) + rs_r[nh - 2].astype(F32) + rs_r[2 * nh - 1].astype(F32)
            first = c == 0
            ctx[:, pl.ds(half_lane, half)] = jnp.where(first, total[:sdev], total[sdev:])
            ctx_s[...] = jnp.where(first, total[sdev:], total[:sdev])
            copy_to(ctx_s, ctx.at[:, pl.ds(half_lane, half)], ex_s.at[2], ex_r.at[2], other).start()

        @pl.when(i < nh)
        def _():
            w_z(0, i, c)(i).wait_recv()

            @pl.when(i > 0)
            def _():
                w_z(1, i, c)(i).wait_recv()

            @pl.when(i < nh - 1)
            def _():
                w_z(0, i, c)(i + 1).start()
                w_z(1, i, c)(i + 1).start()

            for d in (0, 1):
                for side in (0, 1):
                    w_x1(d, side, i).start()

        @pl.when(jnp.logical_and(i >= lag, i < nh + lag))
        def _():
            for d in (0, 1):
                for side in (0, 1):
                    w_x1(d, side, i - lag).wait_recv()
            for d in (0, 1):
                w_x2(d, i - lag).start()

        @pl.when(jnp.logical_and(i >= 2 * lag, i < nh + 2 * lag))
        def _():
            for d in (0, 1):
                w_x2(d, i - 2 * lag).wait_recv()
                w_y(d, i - 2 * lag).start()

        @pl.when(i >= 3 * lag)
        def _():
            for d in (0, 1):
                w_y(d, i - 3 * lag).wait_recv()
                w_c(d, i - 3 * lag, c).start()

        @pl.when(i < first_send)
        def _():
            lax.fori_loop(2 * i, jnp.minimum(2 * i + 2, levels), lookup, 0)

        @pl.when(i == first_send - 1)
        def _():
            rr[mp] = yb[mp]

        @pl.when(i == first_send)
        def _():
            a2a(z * 2 + o).start()
            for cc in (0, 1):
                leg_one(cc).start()
            temporal_t[...] = temporal[...].astype(F32).T.astype(BF16)

        @pl.when(i == nh - 1)
        def _():
            for cc in (0, 1):
                await_leg(cc)
                leg_two(cc).start()

        @pl.when(jnp.logical_and(i >= first_send, i < nh))
        def _():
            for e in (0, 1):
                apart = nh - 2 * (i - first_send) - e

                @pl.when(apart < nh)
                def _():
                    for cc in (0, 1):
                        a2a(wrap(z + apart, nz) * 2 + cc).start()
                        a2a(wrap(z - apart, nz) * 2 + cc).start()

        return carry

    lax.fori_loop(0, nh + 3 * lag, early, 0)

    def await_w(k, carry):
        for d in (0, 1):
            w_c(d, k, o).wait_recv()
        return carry

    fchunk = 256 if ff % 512 == 0 else 128
    near = ff // fchunk // 2

    def hidden_back(k, carry):
        at = pl.ds(pl.multiple_of(k * fchunk, fchunk), fchunk)
        hback[:, at] = dot_t(out_grad[...], wall[2, at, :])
        return carry

    lax.fori_loop(c * near, c * near + near, hidden_back, 0)
    lax.fori_loop(0, nh, await_w, 0)
    lax.fori_loop(o * near, o * near + near, hidden_back, 0)

    def await_a2a(k, carry):
        copy_to(yb.at[k], rr.at[k], a2a_s.at[k], a2a_r.at[k], other).wait_recv()
        return carry

    lax.fori_loop(0, mp, await_a2a, 0)
    lax.fori_loop(mp + 1, n_mp, await_a2a, 0)
    copy_to(ctx_s, ctx.at[:, pl.ds(other_lane, half)], ex_s.at[2], ex_r.at[2], other).wait_recv()

    p_row = lax.broadcasted_iota(jnp.int32, (rows, 256), 0)
    p_col = lax.broadcasted_iota(jnp.int32, (rows, 256), 1)
    p_lane = (jnp.bitwise_and(p_row, 7) - 1) * 32 + lax.shift_right_logical(p_row, 3)
    place = (p_lane == p_col).astype(F32).astype(BF16)

    def place_rows(k, carry):
        at = pl.ds(pl.multiple_of(k * 8, 8), 8)
        sides = []
        for h in range(2):
            tiles = [
                rr[at, l].astype(F32).reshape(64, LANES) if l < levels else jnp.zeros((64, LANES), F32)
                for l in range(4 * h, 4 * h + 4)
            ]
            tiles = [t.reshape(8, 1, 8, LANES) for t in swap_blocks(tiles)]
            sides.append(jnp.concatenate(tiles, axis=1).reshape(256, LANES))
        block = jnp.concatenate(sides, axis=1).astype(BF16)
        inp[:, pl.ds(pl.multiple_of(k * 256, 256), 256)] = dot_t(place, block)
        return carry

    lax.fori_loop(0, n_mp // 8, place_rows, 0)

    part = 64

    def normalise(k, carry):
        at = pl.ds(pl.multiple_of(k * part, part), part)
        base = ctx[pl.ds(pl.multiple_of(k * (part // 8), 8), part // 8), :]
        value = inp[at, :] + jnp.broadcast_to(base[:, None, :], (part // 8, 8, width)).reshape(part, width)
        scale = lax.rsqrt(jnp.mean(value * value, axis=-1, keepdims=True) + 1e-06)
        normed = value * scale
        inp[at, :] = value
        nrm[at, :] = normed
        nlow[at, :] = normed.astype(BF16)
        inv[at, :] = jnp.broadcast_to(scale, (part, LANES))
        ngrad[at, :] = jnp.zeros((part, width), F32)
        return carry

    lax.fori_loop(0, rows // part, normalise, 0)

    def depth(k, carry):
        at = pl.ds(pl.multiple_of(k * fchunk, fchunk), fchunk)
        gate = dot_t(nlow[...], wall[0, at, :])
        upper = dot_t(nlow[...], wall[1, at, :])
        hgrad = hback[:, at]
        sig = jax.nn.sigmoid(gate)
        act = gate * sig
        hid[:, at] = (act * upper).astype(BF16)
        ggrad = (hgrad * upper * sig * (1.0 + gate * (1.0 - sig))).astype(BF16)
        ugrad = (hgrad * act).astype(BF16)
        ngrad[...] += dot(ggrad, wall[0, at, :]) + dot(ugrad, wall[1, at, :])
        return carry

    lax.fori_loop(0, ff // fchunk, depth, 0)

    part_g = sdev // 2

    def g_rows(zs, cc, first, count):
        return cback.at[pl.ds(pl.multiple_of((wrap(zs, nz) * 2 + cc) * sdev + first, 16), count), :]

    def g_z(d, i, k, h):
        block = g_rows(origin(d, i), c, h * part_g, part_g)
        at = (d * nh + k) * 2 + h
        return copy_to(block, block, gz_s.at[at], gz_r.at[at], zp if d == 0 else zm)

    def g_c(d, i, cc):
        block = g_rows(origin(d, i), cc, 0, sdev)
        return copy_to(block, block, gc_s.at[d * nh + i], gc_r.at[d * nh + i], other)

    def back(k, carry):
        at = pl.ds(pl.multiple_of(k * (rows // 2), rows // 2), rows // 2)
        grad, normed = ngrad[at, :], nrm[at, :]
        inner = jnp.mean(grad * normed, axis=-1, keepdims=True)
        total = out_grad[at, :].astype(F32) + inv[at, :1] * (grad - normed * inner)
        summed = jnp.sum(total.reshape(part_g, 8, width), axis=1)
        cback[pl.ds(pl.multiple_of(mp * sdev + k * part_g, 16), part_g), :] = summed.astype(BF16)
        g_z(0, -1, 0, k).start()
        g_z(1, 0, 1, k).start()
        return carry

    lax.fori_loop(0, 2, back, 0)

    inv_n = 1.0 / steps

    def sent_early(i):
        w_z(0, i, c)(i).wait_send()
        ring_sum(1, i).wait_send()

        @pl.when(i > 0)
        def _():
            w_z(1, i, c)(i).wait_send()

        @pl.when(i < nh - 1)
        def _():
            ring_sum(0, i).wait_send()

        for d in (0, 1):
            for side in (0, 1):
                w_x1(d, side, i).wait_send()
            w_x2(d, i).wait_send()
            w_y(d, i).wait_send()
            w_c(d, i, c).wait_send()

        def sent_a2a(k, carry):
            a2a(lax.rem(mp + k, n_mp)).wait_send()
            return carry

        lax.fori_loop(1 + 4 * i, jnp.minimum(5 + 4 * i, n_mp), sent_a2a, 0)

    ex_t.wait_send()
    ex_w.wait_send()
    copy_to(ctx_s, ctx.at[:, pl.ds(half_lane, half)], ex_s.at[2], ex_r.at[2], other).wait_send()
    for cc in (0, 1):
        leg_two(cc).wait_send()
    n_chunks = width // 256

    def late(i, carry):
        for h in (0, 1):

            @pl.when(i > 0)
            def _():
                g_z(0, i - 1, i - 1, h).wait_recv()

                @pl.when(i < nh)
                def _():
                    g_z(0, i - 1, i, h).start()

            @pl.when(jnp.logical_and(i > 0, i < nh))
            def _():
                g_z(1, i, i, h).wait_recv()

                @pl.when(i < nh - 1)
                def _():
                    g_z(1, i, i + 1, h).start()

        @pl.when(i > 0)
        def _():
            g_c(0, i - 1, c).start()

        @pl.when(i < nh)
        def _():
            g_c(1, i, c).start()

        @pl.when(i < n_chunks)
        def _():
            at = pl.ds(pl.multiple_of(i * 256, 256), 256)
            out[:, at] = (inp[:, at] + dot(hid[...], wall[2, :, at])).astype(BF16)

        @pl.when(i < nh)
        def _():
            sent_early(i)

        return carry

    lax.fori_loop(0, nh + 1, late, 0)

    def await_g(k, carry):
        for d in (0, 1):
            g_c(d, k, o).wait_recv()
        return carry

    lax.fori_loop(0, nh, await_g, 0)

    cols = width // n_dp
    cg_s[...] = (dot(temporal_t[...], cback[...]) * inv_n).T.astype(BF16)

    def cg(target):
        block = cg_s.at[pl.ds(pl.multiple_of(target * cols, 16), cols), :]
        return copy_to(block, cg_r.at[dp], dp_s.at[target], dp_r.at[dp], (target, mp))

    def send_cg(k, carry):
        cg(lax.rem(dp + k, n_dp)).start()
        return carry

    lax.fori_loop(1, n_dp, send_cg, 0)
    cg_r[dp] = cg_s[pl.ds(pl.multiple_of(dp * cols, 16), cols), :]

    def tgrad(k, carry):
        at = pl.ds(pl.multiple_of(k * chunk, chunk), chunk)
        temporal_grad[at, :] = dot_t(cback[at, :], ctx_weight[...]).astype(BF16)
        return carry

    lax.fori_loop(0, steps // chunk, tgrad, 0)

    def sent(i, carry):
        for h in (0, 1):
            g_z(0, i, i, h).wait_send()

        @pl.when(i > 0)
        def _():
            for h in (0, 1):
                g_z(1, i, i, h).wait_send()

        for d in (0, 1):
            g_c(d, i, c).wait_send()
        return carry

    lax.fori_loop(0, nh, sent, 0)

    def await_cg(k, carry):
        source = lax.rem(dp + k, n_dp)
        copy_to(cg_r.at[source], cg_r.at[source], dp_s.at[source], dp_r.at[source], other).wait_recv()
        cg(source).wait_send()
        return carry

    lax.fori_loop(1, n_dp, await_cg, 0)
    total = cg_r[0].astype(F32)
    for k in range(1, n_dp):
        total = total + cg_r[k].astype(F32)
    context_grad[...] = total


def hand_over(a, b, d, a_out, b_out, d_out):
    a_out[...] = a[...]
    b_out[...] = b[...]
    d_out[...] = d[...]


def per_device(
    n_dp, n_mp, temporal, code_ids, context_weight, code_tables, gate_proj, up_proj, down_proj, out_grad
):
    steps, feat = temporal.shape
    sdev, levels, width = out_grad.shape
    rows = sdev * levels
    unit = down_proj.shape[0]
    ff = unit * n_mp
    nh = n_mp // 4
    cols = width // n_dp
    half = width // 2
    inputs_levels = code_tables.shape[0]
    vmem = pl.BlockSpec(memory_space=pltpu.VMEM)
    dma = lambda n: pltpu.SemaphoreType.DMA((n,))
    scratch = [
        pltpu.VMEM((3, ff, width), BF16),
        pltpu.VMEM((steps, 2 * feat), BF16),
        pltpu.VMEM((2 * feat, half), BF16),
        pltpu.VMEM((steps, half), F32),
        pltpu.VMEM((2 * nh, 2 * sdev, half), BF16),
        pltpu.VMEM((2 * nh, 2 * sdev, half), BF16),
        pltpu.VMEM((n_mp, inputs_levels, 8, LANES), BF16),
        pltpu.VMEM((n_mp, inputs_levels, 8, LANES), BF16),
        pltpu.VMEM((2, inputs_levels, 8, LANES), BF16),
        pltpu.VMEM((sdev, width), F32),
        pltpu.VMEM((sdev, half), F32),
        pltpu.VMEM((feat, steps), BF16),
        pltpu.VMEM((rows, width), F32),
        pltpu.VMEM((rows, width), F32),
        pltpu.VMEM((rows, width), BF16),
        pltpu.VMEM((rows, LANES), F32),
        pltpu.VMEM((rows, ff), BF16),
        pltpu.VMEM((rows, ff), F32),
        pltpu.VMEM((rows, width), F32),
        pltpu.VMEM((steps, width), BF16),
        pltpu.VMEM((width, feat), BF16),
        pltpu.VMEM((n_dp, cols, feat), BF16),
    ]
    sems = [2 * nh, 4 * nh, 2 * nh, 2 * nh, 2 * nh, 2 * nh, n_mp, 4 * nh, 2 * nh, n_dp, 3, 2]
    for n in sems:
        scratch += [dma(n), dma(n)]
    out, tgrad, cgrad = pl.pallas_call(
        functools.partial(kernel, n_dp, n_mp),
        out_shape=(
            jax.ShapeDtypeStruct((rows, width), BF16),
            jax.ShapeDtypeStruct((steps, feat), BF16),
            jax.ShapeDtypeStruct((cols, feat), F32),
        ),
        in_specs=[vmem] * 8,
        out_specs=(vmem, vmem, vmem),
        scratch_shapes=scratch,
        compiler_params=pltpu.CompilerParams(
            collective_id=0, has_side_effects=True, vmem_limit_bytes=58 * 1024 * 1024
        ),
        cost_estimate=pl.CostEstimate(
            flops=2 * rows * width * ff * 6 + 6 * steps * feat * width, bytes_accessed=4 * 2**20, transcendentals=0
        ),
        name="depth_block",
    )(
        temporal,
        code_ids.T,
        context_weight,
        code_tables.transpose(0, 2, 1),
        gate_proj.T,
        up_proj.T,
        down_proj,
        out_grad.reshape(rows, width),
    )
    out, tgrad, cgrad = pl.pallas_call(
        hand_over,
        out_shape=tuple(jax.ShapeDtypeStruct(v.shape, v.dtype) for v in (out, tgrad, cgrad)),
        in_specs=[vmem] * 3,
        out_specs=(vmem,) * 3,
        name="hand_over",
    )(out, tgrad, cgrad)
    return out.reshape(sdev, levels, width), tgrad, cgrad.T


def solution(mesh):
    in_specs = (
        P("dp", "mp"),
        P("dp", None),
        P("mp", None),
        P(None, None, "mp"),
        P(None, "mp"),
        P(None, "mp"),
        P("mp", None),
        P(("dp", "mp"), None, None),
    )
    out_specs = (P(("dp", "mp"), None, None), P("dp", "mp"), P("mp", "dp"))
    return jax.shard_map(
        functools.partial(per_device, mesh.shape["dp"], mesh.shape["mp"]),
        mesh=mesh,
        in_specs=in_specs,
        out_specs=out_specs,
        check_vma=False,
    )
```

```python
import functools

import jax
import jax.numpy as jnp
from jax import lax
from jax.experimental import pallas as pl
from jax.experimental.pallas import tpu as pltpu
from jax.sharding import PartitionSpec as P

NX = 4
LANES = 128
BF16 = jnp.bfloat16
F32 = jnp.float32
MESH = pl.DeviceIdType.MESH


def dot_t(left, right):
    return lax.dot_general(left, right, (((1,), (1,)), ((), ())), preferred_element_type=F32)


def dot(left, right):
    return lax.dot_general(left, right, (((1,), (0,)), ((), ())), preferred_element_type=F32)


def copy_to(src, dst, send, recv, device):
    return pltpu.make_async_remote_copy(
        src_ref=src, dst_ref=dst, send_sem=send, recv_sem=recv, device_id=device, device_id_type=MESH
    )


def swap_blocks(v):
    lane = lax.broadcasted_iota(jnp.int32, v[0].shape, 1)
    low = lane < 64
    even = jnp.bitwise_and(lane, 32) == 0
    w = [None] * 4
    for a in (0, 1):
        w[a] = jnp.where(low, v[a], pltpu.roll(v[a + 2], 64, 1))
        w[a + 2] = jnp.where(low, pltpu.roll(v[a], 64, 1), v[a + 2])
    out = [None] * 4
    for a in (0, 2):
        out[a] = jnp.where(even, w[a], pltpu.roll(w[a + 1], 32, 1))
        out[a + 1] = jnp.where(even, pltpu.roll(w[a], 96, 1), w[a + 1])
    return out


def kernel(
    n_dp, n_mp,
    temporal, codes, ctx_weight, tables, gate_t, up_t, down, out_grad,
    out, temporal_grad, context_grad,
    wall, tx, wx, sums, rs_s, rs_r, yb, rr, relay, ctx, ctx_s, temporal_t,
    inp, nrm, nlow, inv, hid, hback, ngrad, cback, cg_s, cg_r,
    z_s, z_r, x1_s, x1_r, x2_s, x2_r, y_s, y_r, c_s, c_r, rsum_s, rsum_r,
    a2a_s, a2a_r, gz_s, gz_r, gc_s, gc_r, dp_s, dp_r, ex_s, ex_r, rl_s, rl_r,
):
    nz = n_mp // 2
    nh = nz // 2
    ny = n_dp // NX
    dp, mp = lax.axis_index("dp"), lax.axis_index("mp")
    x, y = lax.rem(dp, NX), lax.div(dp, NX)
    z, c = lax.div(mp, 2), lax.rem(mp, 2)
    o = 1 - c
    par = lax.rem(y, 2)
    steps = temporal.shape[0]
    sdev = steps // n_mp
    width = ctx_weight.shape[1]
    half = width // 2
    rows = 8 * sdev
    unit = gate_t.shape[0]
    ff = wall.shape[1]

    def wrap(v, n):
        return lax.rem(v + 2 * n, n)

    def at_z(zz, cc):
        return (dp, wrap(zz, nz) * 2 + cc)

    def at_plane(yy, xx):
        return (wrap(yy, ny) * NX + wrap(xx, NX), mp)

    zp, zm = at_z(z + 1, c), at_z(z - 1, c)
    xp, xm = at_plane(y, x + 1), at_plane(y, x - 1)
    yp, ym = at_plane(y + 1, x), at_plane(y - 1, x)
    other = (dp, z * 2 + o)

    barrier = pltpu.get_barrier_semaphore()

    def greet_mp(k, carry):
        pl.semaphore_signal(barrier, inc=1, device_id=(dp, lax.rem(mp + k, n_mp)), device_id_type=MESH)
        return carry

    def greet_dp(k, carry):
        pl.semaphore_signal(barrier, inc=1, device_id=(lax.rem(dp + k, n_dp), mp), device_id_type=MESH)
        return carry

    lax.fori_loop(1, n_mp, greet_mp, 0)
    lax.fori_loop(1, n_dp, greet_dp, 0)

    def w_at(cc, zs, lane, count):
        row = pl.multiple_of((cc * nz + wrap(zs, nz)) * unit, 16)
        return wall.at[:, pl.ds(row, unit), pl.ds(pl.multiple_of(lane, LANES), count)]

    def tile_of(xx):
        return (par * NX + wrap(xx, NX)) * LANES

    mine = tile_of(x)
    row0 = pl.multiple_of((c * nz + z) * unit, 16)
    lane0 = pl.multiple_of(mine, LANES)
    for index, shard in enumerate((gate_t, up_t, down)):
        wall[index, pl.ds(row0, unit), pl.ds(lane0, LANES)] = shard[:, pl.ds(lane0, LANES)]

    pl.semaphore_wait(barrier, n_mp - 1 + n_dp - 1)

    def origin(d, i):
        return z - 1 - i if d == 0 else z + i

    def w_z(d, i, cc):
        zs = origin(d, i)
        return lambda k: copy_to(
            w_at(cc, zs, mine, LANES), w_at(cc, zs, mine, LANES), z_s.at[d * nh + k], z_r.at[d * nh + k],
            zp if d == 0 else zm,
        )

    half_lane = pl.multiple_of(c * half, LANES)
    other_lane = pl.multiple_of(o * half, LANES)
    feat = temporal.shape[1]
    own_feat = pl.multiple_of(c * feat, LANES)
    ex_t = copy_to(temporal, tx.at[:, pl.ds(own_feat, feat)], ex_s.at[0], ex_r.at[0], other)
    ex_w = copy_to(
        ctx_weight.at[:, pl.ds(other_lane, half)], wx.at[pl.ds(own_feat, feat), :], ex_s.at[1], ex_r.at[1], other
    )
    ex_t.start()
    ex_w.start()
    w_z(0, -1, c)(0).start()
    tx[:, pl.ds(own_feat, feat)] = temporal[...]
    wx[pl.ds(own_feat, feat), :] = ctx_weight[:, pl.ds(half_lane, half)]


    def lookup(level, carry):
        code = codes[pl.ds(level, 1), :]
        low = jnp.bitwise_and(code, 255)
        high = lax.shift_right_logical(code, 8)
        table = tables[level]
        parts = table.shape[1] // 256
        stacked = jnp.concatenate([table[:, a * 256 : (a + 1) * 256] for a in range(parts)], axis=0)
        per = min(256, steps)
        for q in range(steps // per):
            piece = slice(q * per, (q + 1) * per)
            hot = (lax.broadcasted_iota(jnp.int32, (256, per), 0) == low[:, piece]).astype(F32).astype(BF16)
            picked = dot(stacked, hot)
            total = jnp.zeros((fsize, per), F32)
            for a in range(parts):
                total = total + jnp.where(high[:, piece] == a, picked[a * fsize : (a + 1) * fsize, :], 0.0)
            for e in range(per // LANES):
                g = q * (per // LANES) + e
                block = total[:, e * LANES : (e + 1) * LANES]
                tiles = swap_blocks([block[8 * a : 8 * a + 8] for a in range(4)])
                for a in range(4):
                    yb[4 * g + a, level] = tiles[a].astype(BF16)
        return carry

    levels = codes.shape[0]
    fsize = tables.shape[1]

    def a2a(target):
        return copy_to(yb.at[target], rr.at[mp], a2a_s.at[target], a2a_r.at[mp], (dp, target))

    quarter = nh // 2

    def leg_one(cc):
        target = wrap(z + nh, nz) * 2 + cc
        over = z + quarter if cc == 0 else z - quarter
        return copy_to(yb.at[target], relay.at[cc], a2a_s.at[target], rl_r.at[cc], at_z(over, c))

    def leg_two(cc):
        source, over = (z - quarter, z + quarter) if cc == 0 else (z + quarter, z - quarter)
        origin_mp = wrap(source, nz) * 2 + c
        return copy_to(relay.at[cc], rr.at[origin_mp], rl_s.at[cc], a2a_r.at[origin_mp], at_z(over, cc))

    def await_leg(cc):
        copy_to(relay.at[cc], relay.at[cc], rl_s.at[cc], rl_r.at[cc], other).wait_recv()

    ex_t.wait_recv()
    ex_w.wait_recv()
    chunk = min(256, steps)

    def term(k, carry):
        at = pl.ds(pl.multiple_of(k * chunk, chunk), chunk)
        sums[at, :] = dot(tx[at, :], wx[...])
        return carry

    lax.fori_loop(0, steps // chunk, term, 0)

    chip = 2 * sdev

    def term_of(zd):
        return sums[pl.ds(pl.multiple_of(wrap(zd, nz) * chip, 16), chip), :]

    def ring_sum(d, i):
        k = d * nh + i
        return copy_to(rs_s.at[k], rs_r.at[k], rsum_s.at[k], rsum_r.at[k], zp if d == 0 else zm)

    def dest(d, i):
        return z + (nh - 1) - i if d == 0 else z - nh + i

    for d in (0, 1):
        rs_s[d * nh] = term_of(dest(d, 0)).astype(BF16)
        ring_sum(d, 0).start()

    def w_x1(d, side, i):
        k = (d * 2 + side) * nh + i
        block = w_at(c, origin(d, i), mine, LANES)
        return copy_to(block, block, x1_s.at[k], x1_r.at[k], xp if side == 0 else xm)

    def w_x2(d, i):
        block = w_at(c, origin(d, i), tile_of(x - 1 if d == 0 else x + 1), LANES)
        return copy_to(block, block, x2_s.at[d * nh + i], x2_r.at[d * nh + i], xp if d == 0 else xm)

    def w_y(d, i):
        block = w_at(c, origin(d, i), par * NX * LANES, NX * LANES)
        return copy_to(block, block, y_s.at[d * nh + i], y_r.at[d * nh + i], yp if d == 0 else ym)

    def w_c(d, i, cc):
        block = w_at(cc, origin(d, i), 0, width)
        return copy_to(block, block, c_s.at[d * nh + i], c_r.at[d * nh + i], other)

    first_send = nh // 2
    lag = 2

    def early(i, carry):
        for d in (0, 1):
            last = nh - 2 if d == 0 else nh - 1

            @pl.when(i < last)
            def _():
                ring_sum(d, i).wait_recv()
                rs_s[d * nh + i + 1] = (
                    term_of(dest(d, i + 1)) + rs_r[d * nh + i].astype(F32)
                ).astype(BF16)
                ring_sum(d, i + 1).start()

        @pl.when(i == nh)
        def _():
            ring_sum(0, nh - 2).wait_recv()
            ring_sum(1, nh - 1).wait_recv()
            total = term_of(z) + rs_r[nh - 2].astype(F32) + rs_r[2 * nh - 1].astype(F32)
            first = c == 0
            ctx[:, pl.ds(half_lane, half)] = jnp.where(first, total[:sdev], total[sdev:])
            ctx_s[...] = jnp.where(first, total[sdev:], total[:sdev])
            copy_to(ctx_s, ctx.at[:, pl.ds(half_lane, half)], ex_s.at[2], ex_r.at[2], other).start()

        @pl.when(i < nh)
        def _():
            w_z(0, i, c)(i).wait_recv()

            @pl.when(i > 0)
            def _():
                w_z(1, i, c)(i).wait_recv()

            @pl.when(i < nh - 1)
            def _():
                w_z(0, i, c)(i + 1).start()
                w_z(1, i, c)(i + 1).start()

            for d in (0, 1):
                for side in (0, 1):
                    w_x1(d, side, i).start()

        @pl.when(jnp.logical_and(i >= lag, i < nh + lag))
        def _():
            for d in (0, 1):
                for side in (0, 1):
                    w_x1(d, side, i - lag).wait_recv()
            for d in (0, 1):
                w_x2(d, i - lag).start()

        @pl.when(jnp.logical_and(i >= 2 * lag, i < nh + 2 * lag))
        def _():
            for d in (0, 1):
                w_x2(d, i - 2 * lag).wait_recv()
                w_y(d, i - 2 * lag).start()

        @pl.when(i >= 3 * lag)
        def _():
            for d in (0, 1):
                w_y(d, i - 3 * lag).wait_recv()
                w_c(d, i - 3 * lag, c).start()

        @pl.when(i < first_send)
        def _():
            lax.fori_loop(2 * i, jnp.minimum(2 * i + 2, levels), lookup, 0)

        @pl.when(i == first_send - 1)
        def _():
            rr[mp] = yb[mp]

        @pl.when(i == first_send)
        def _():
            a2a(z * 2 + o).start()
            for cc in (0, 1):
                leg_one(cc).start()
            temporal_t[...] = temporal[...].astype(F32).T.astype(BF16)

        @pl.when(i == nh - 1)
        def _():
            for cc in (0, 1):
                await_leg(cc)
                leg_two(cc).start()

        @pl.when(jnp.logical_and(i >= first_send, i < nh))
        def _():
            for e in (0, 1):
                apart = nh - 2 * (i - first_send) - e

                @pl.when(apart < nh)
                def _():
                    for cc in (0, 1):
                        a2a(wrap(z + apart, nz) * 2 + cc).start()
                        a2a(wrap(z - apart, nz) * 2 + cc).start()

        return carry

    lax.fori_loop(0, nh + 3 * lag, early, 0)

    def await_w(k, carry):
        for d in (0, 1):
            w_c(d, k, o).wait_recv()
        return carry

    fchunk = 256 if ff % 512 == 0 else 128
    near = ff // fchunk // 2

    def hidden_back(k, carry):
        at = pl.ds(pl.multiple_of(k * fchunk, fchunk), fchunk)
        hback[:, at] = dot_t(out_grad[...], wall[2, at, :])
        return carry

    lax.fori_loop(c * near, c * near + near, hidden_back, 0)
    lax.fori_loop(0, nh, await_w, 0)
    lax.fori_loop(o * near, o * near + near, hidden_back, 0)

    def await_a2a(k, carry):
        copy_to(yb.at[k], rr.at[k], a2a_s.at[k], a2a_r.at[k], other).wait_recv()
        return carry

    lax.fori_loop(0, mp, await_a2a, 0)
    lax.fori_loop(mp + 1, n_mp, await_a2a, 0)
    copy_to(ctx_s, ctx.at[:, pl.ds(other_lane, half)], ex_s.at[2], ex_r.at[2], other).wait_recv()

    p_row = lax.broadcasted_iota(jnp.int32, (rows, 256), 0)
    p_col = lax.broadcasted_iota(jnp.int32, (rows, 256), 1)
    p_lane = (jnp.bitwise_and(p_row, 7) - 1) * 32 + lax.shift_right_logical(p_row, 3)
    place = (p_lane == p_col).astype(F32).astype(BF16)

    def place_rows(k, carry):
        at = pl.ds(pl.multiple_of(k * 8, 8), 8)
        sides = []
        for h in range(2):
            tiles = [
                rr[at, l].astype(F32).reshape(64, LANES) if l < levels else jnp.zeros((64, LANES), F32)
                for l in range(4 * h, 4 * h + 4)
            ]
            tiles = [t.reshape(8, 1, 8, LANES) for t in swap_blocks(tiles)]
            sides.append(jnp.concatenate(tiles, axis=1).reshape(256, LANES))
        block = jnp.concatenate(sides, axis=1).astype(BF16)
        inp[:, pl.ds(pl.multiple_of(k * 256, 256), 256)] = dot_t(place, block)
        return carry

    lax.fori_loop(0, n_mp // 8, place_rows, 0)

    part = 64

    def normalise(k, carry):
        at = pl.ds(pl.multiple_of(k * part, part), part)
        base = ctx[pl.ds(pl.multiple_of(k * (part // 8), 8), part // 8), :]
        value = inp[at, :] + jnp.broadcast_to(base[:, None, :], (part // 8, 8, width)).reshape(part, width)
        scale = lax.rsqrt(jnp.mean(value * value, axis=-1, keepdims=True) + 1e-06)
        normed = value * scale
        inp[at, :] = value
        nrm[at, :] = normed
        nlow[at, :] = normed.astype(BF16)
        inv[at, :] = jnp.broadcast_to(scale, (part, LANES))
        ngrad[at, :] = jnp.zeros((part, width), F32)
        return carry

    lax.fori_loop(0, rows // part, normalise, 0)

    wide = 512 if ff % 512 == 0 else fchunk

    def depth(k, carry):
        at = pl.ds(pl.multiple_of(k * wide, wide), wide)
        gate = dot_t(nlow[...], wall[0, at, :])
        upper = dot_t(nlow[...], wall[1, at, :])
        hgrad = hback[:, at]
        sig = jax.nn.sigmoid(gate)
        act = gate * sig
        hid[:, at] = (act * upper).astype(BF16)
        ggrad = (hgrad * upper * sig * (1.0 + gate * (1.0 - sig))).astype(BF16)
        ugrad = (hgrad * act).astype(BF16)
        ngrad[...] += dot(ggrad, wall[0, at, :]) + dot(ugrad, wall[1, at, :])
        return carry

    lax.fori_loop(0, ff // wide, depth, 0)

    part_g = sdev // 2

    def g_rows(zs, cc, first, count):
        return cback.at[pl.ds(pl.multiple_of((wrap(zs, nz) * 2 + cc) * sdev + first, 16), count), :]

    def g_z(d, i, k, h):
        block = g_rows(origin(d, i), c, h * part_g, part_g)
        at = (d * nh + k) * 2 + h
        return copy_to(block, block, gz_s.at[at], gz_r.at[at], zp if d == 0 else zm)

    def g_c(d, i, cc):
        block = g_rows(origin(d, i), cc, 0, sdev)
        return copy_to(block, block, gc_s.at[d * nh + i], gc_r.at[d * nh + i], other)

    def back(k, carry):
        at = pl.ds(pl.multiple_of(k * (rows // 2), rows // 2), rows // 2)
        grad, normed = ngrad[at, :], nrm[at, :]
        inner = jnp.mean(grad * normed, axis=-1, keepdims=True)
        total = out_grad[at, :].astype(F32) + inv[at, :1] * (grad - normed * inner)
        summed = jnp.sum(total.reshape(part_g, 8, width), axis=1)
        cback[pl.ds(pl.multiple_of(mp * sdev + k * part_g, 16), part_g), :] = summed.astype(BF16)
        g_z(0, -1, 0, k).start()
        g_z(1, 0, 1, k).start()
        return carry

    lax.fori_loop(0, 2, back, 0)

    inv_n = 1.0 / steps

    def sent_early(i):
        w_z(0, i, c)(i).wait_send()
        ring_sum(1, i).wait_send()

        @pl.when(i > 0)
        def _():
            w_z(1, i, c)(i).wait_send()

        @pl.when(i < nh - 1)
        def _():
            ring_sum(0, i).wait_send()

        for d in (0, 1):
            for side in (0, 1):
                w_x1(d, side, i).wait_send()
            w_x2(d, i).wait_send()
            w_y(d, i).wait_send()
            w_c(d, i, c).wait_send()

        def sent_a2a(k, carry):
            a2a(lax.rem(mp + k, n_mp)).wait_send()
            return carry

        lax.fori_loop(1 + 4 * i, jnp.minimum(5 + 4 * i, n_mp), sent_a2a, 0)

    ex_t.wait_send()
    ex_w.wait_send()
    copy_to(ctx_s, ctx.at[:, pl.ds(half_lane, half)], ex_s.at[2], ex_r.at[2], other).wait_send()
    for cc in (0, 1):
        leg_two(cc).wait_send()
    n_chunks = width // 256

    def late(i, carry):
        for h in (0, 1):

            @pl.when(i > 0)
            def _():
                g_z(0, i - 1, i - 1, h).wait_recv()

                @pl.when(i < nh)
                def _():
                    g_z(0, i - 1, i, h).start()

            @pl.when(jnp.logical_and(i > 0, i < nh))
            def _():
                g_z(1, i, i, h).wait_recv()

                @pl.when(i < nh - 1)
                def _():
                    g_z(1, i, i + 1, h).start()

        @pl.when(i > 0)
        def _():
            g_c(0, i - 1, c).start()

        @pl.when(i < nh)
        def _():
            g_c(1, i, c).start()

        @pl.when(i < n_chunks)
        def _():
            at = pl.ds(pl.multiple_of(i * 256, 256), 256)
            out[:, at] = (inp[:, at] + dot(hid[...], wall[2, :, at])).astype(BF16)

        @pl.when(i < nh)
        def _():
            sent_early(i)

        return carry

    lax.fori_loop(0, nh + 1, late, 0)

    def await_g(k, carry):
        for d in (0, 1):
            g_c(d, k, o).wait_recv()
        return carry

    lax.fori_loop(0, nh, await_g, 0)

    cols = width // n_dp
    cg_s[...] = (dot(temporal_t[...], cback[...]) * inv_n).T.astype(BF16)

    def cg(target):
        block = cg_s.at[pl.ds(pl.multiple_of(target * cols, 16), cols), :]
        return copy_to(block, cg_r.at[dp], dp_s.at[target], dp_r.at[dp], (target, mp))

    def send_cg(k, carry):
        cg(lax.rem(dp + k, n_dp)).start()
        return carry

    lax.fori_loop(1, n_dp, send_cg, 0)
    cg_r[dp] = cg_s[pl.ds(pl.multiple_of(dp * cols, 16), cols), :]

    def tgrad(k, carry):
        at = pl.ds(pl.multiple_of(k * chunk, chunk), chunk)
        temporal_grad[at, :] = dot_t(cback[at, :], ctx_weight[...]).astype(BF16)
        return carry

    lax.fori_loop(0, steps // chunk, tgrad, 0)

    def sent(i, carry):
        for h in (0, 1):
            g_z(0, i, i, h).wait_send()

        @pl.when(i > 0)
        def _():
            for h in (0, 1):
                g_z(1, i, i, h).wait_send()

        for d in (0, 1):
            g_c(d, i, c).wait_send()
        return carry

    lax.fori_loop(0, nh, sent, 0)

    def await_cg(k, carry):
        source = lax.rem(dp + k, n_dp)
        copy_to(cg_r.at[source], cg_r.at[source], dp_s.at[source], dp_r.at[source], other).wait_recv()
        cg(source).wait_send()
        return carry

    lax.fori_loop(1, n_dp, await_cg, 0)
    total = cg_r[0].astype(F32)
    for k in range(1, n_dp):
        total = total + cg_r[k].astype(F32)
    context_grad[...] = total


def hand_over(a, b, d, a_out, b_out, d_out):
    a_out[...] = a[...]
    b_out[...] = b[...]
    d_out[...] = d[...]


def per_device(
    n_dp, n_mp, temporal, code_ids, context_weight, code_tables, gate_proj, up_proj, down_proj, out_grad
):
    steps, feat = temporal.shape
    sdev, levels, width = out_grad.shape
    rows = sdev * levels
    unit = down_proj.shape[0]
    ff = unit * n_mp
    nh = n_mp // 4
    cols = width // n_dp
    half = width // 2
    inputs_levels = code_tables.shape[0]
    vmem = pl.BlockSpec(memory_space=pltpu.VMEM)
    dma = lambda n: pltpu.SemaphoreType.DMA((n,))
    scratch = [
        pltpu.VMEM((3, ff, width), BF16),
        pltpu.VMEM((steps, 2 * feat), BF16),
        pltpu.VMEM((2 * feat, half), BF16),
        pltpu.VMEM((steps, half), F32),
        pltpu.VMEM((2 * nh, 2 * sdev, half), BF16),
        pltpu.VMEM((2 * nh, 2 * sdev, half), BF16),
        pltpu.VMEM((n_mp, inputs_levels, 8, LANES), BF16),
        pltpu.VMEM((n_mp, inputs_levels, 8, LANES), BF16),
        pltpu.VMEM((2, inputs_levels, 8, LANES), BF16),
        pltpu.VMEM((sdev, width), F32),
        pltpu.VMEM((sdev, half), F32),
        pltpu.VMEM((feat, steps), BF16),
        pltpu.VMEM((rows, width), F32),
        pltpu.VMEM((rows, width), F32),
        pltpu.VMEM((rows, width), BF16),
        pltpu.VMEM((rows, LANES), F32),
        pltpu.VMEM((rows, ff), BF16),
        pltpu.VMEM((rows, ff), F32),
        pltpu.VMEM((rows, width), F32),
        pltpu.VMEM((steps, width), BF16),
        pltpu.VMEM((width, feat), BF16),
        pltpu.VMEM((n_dp, cols, feat), BF16),
    ]
    sems = [2 * nh, 4 * nh, 2 * nh, 2 * nh, 2 * nh, 2 * nh, n_mp, 4 * nh, 2 * nh, n_dp, 3, 2]
    for n in sems:
        scratch += [dma(n), dma(n)]
    out, tgrad, cgrad = pl.pallas_call(
        functools.partial(kernel, n_dp, n_mp),
        out_shape=(
            jax.ShapeDtypeStruct((rows, width), BF16),
            jax.ShapeDtypeStruct((steps, feat), BF16),
            jax.ShapeDtypeStruct((cols, feat), F32),
        ),
        in_specs=[vmem] * 8,
        out_specs=(vmem, vmem, vmem),
        scratch_shapes=scratch,
        compiler_params=pltpu.CompilerParams(
            collective_id=0, has_side_effects=True, vmem_limit_bytes=58 * 1024 * 1024
        ),
        cost_estimate=pl.CostEstimate(
            flops=2 * rows * width * ff * 6 + 6 * steps * feat * width, bytes_accessed=4 * 2**20, transcendentals=0
        ),
        name="depth_block",
    )(
        temporal,
        code_ids.T,
        context_weight,
        code_tables.transpose(0, 2, 1),
        gate_proj.T,
        up_proj.T,
        down_proj,
        out_grad.reshape(rows, width),
    )
    out, tgrad, cgrad = pl.pallas_call(
        hand_over,
        out_shape=tuple(jax.ShapeDtypeStruct(v.shape, v.dtype) for v in (out, tgrad, cgrad)),
        in_specs=[vmem] * 3,
        out_specs=(vmem,) * 3,
        name="hand_over",
    )(out, tgrad, cgrad)
    return out.reshape(sdev, levels, width), tgrad, cgrad.T


def solution(mesh):
    in_specs = (
        P("dp", "mp"),
        P("dp", None),
        P("mp", None),
        P(None, None, "mp"),
        P(None, "mp"),
        P(None, "mp"),
        P("mp", None),
        P(("dp", "mp"), None, None),
    )
    out_specs = (P(("dp", "mp"), None, None), P("dp", "mp"), P("mp", "dp"))
    return jax.shard_map(
        functools.partial(per_device, mesh.shape["dp"], mesh.shape["mp"]),
        mesh=mesh,
        in_specs=in_specs,
        out_specs=out_specs,
        check_vma=False,
    )
```
